512 devices in a mesh: prow: 32 (over y_lo, z), pcol: 16 (over y_hi, x, core).
Axes of the slice: x: 4, y: 4 (y_hi: 2, y_lo: 2; y = y_hi * 2 + y_lo), z: 16, core: 2. Of those that a mesh axis runs over, the one named last changes fastest.
Arguments:
- matrix: float32 [1, 8192, 2, 4096], P(None, 'prow', None, 'pcol'), may hold values from -6 to 6
- reflectors: float32 [1, 8192, 256], P(None, 'prow'), may hold values from -0.0625 to 0.0625
Outputs:
- updated: float32 [1, 8192, 2, 4096], P(None, 'prow', None, 'pcol')
The draws below stay inside these ranges and needn't reach their ends.
All inputs are finite; a program needn't handle non-finite values.
Results may differ from the reference program's by a relative error of at most 0.0003.
Values sent between devices are 32-bit elements; how exact they have to be, the bound alone decides.
A program may use at most 64 MiB of HBM per device.

```python
import jax
import jax.numpy as jnp
from jax import lax

TILE = 256
RT = 1
CT = 2
N_PROW = 32
N_PCOL = 16


def steps_of(stream_key, dims, cuts, smallest, high):
    def one(dim, blocks):
        heights = jax.random.uniform(jax.random.fold_in(jax.random.fold_in(stream_key, 6), dim), (blocks,), jnp.float32, smallest / len(cuts), high / len(cuts))
        return jnp.repeat(jnp.exp(heights), dims[dim] // blocks).reshape((-1,) + (1,) * (len(dims) - dim - 1))

    factor_of = one(*cuts[0])
    for cut in cuts[1:]:
        factor_of = factor_of * one(*cut)
    return factor_of


def bell_draw(key, dims, width, most, shards=(), kind=jnp.bfloat16):
    loudness = steps_of(key, dims, shards, -0.22, 0.18) if shards else 1.0
    values = jax.random.normal(key, dims, jnp.float32) * width * loudness
    return jnp.minimum(jnp.maximum(values, -most), most).astype(kind)


def setup_inputs(seed: int = 0) -> dict:
    key_of = jax.random.split(jax.random.key(seed), 3)
    return {
        "matrix": bell_draw(key_of[0], (RT, N_PROW * TILE, CT, N_PCOL * TILE), 1.0, 6.0, ((1, 32), (3, 16)), jnp.float32),
        "reflectors": bell_draw(key_of[1], (RT, N_PROW * TILE, TILE), (RT * N_PROW * TILE) ** -0.5, 0.0625, ((1, 32),), jnp.float32),
    }


precise = lax.Precision.HIGHEST


def invert_factor(gram_total):
    order = gram_total.shape[0]
    scale = 0.5 * jnp.diagonal(gram_total)
    nilpotent = jnp.triu(gram_total, 1) / scale[:, None]
    eye_matrix = jnp.eye(order, dtype=gram_total.dtype)
    power = -nilpotent
    result = eye_matrix + power
    exponent = 1
    while exponent < order:
        power = jnp.dot(power, power, precision=precise)
        result = jnp.dot(result, eye_matrix + power, precision=precise)
        exponent = exponent * 2
    return result / scale[None, :]


def reference(matrix, reflectors):
    matrix_order = RT * N_PROW * TILE
    full_matrix = matrix.reshape(matrix_order, matrix_order)
    tile_ids = jnp.arange(matrix_order, dtype=jnp.int32) // TILE
    strict = tile_ids[:, None] > tile_ids[None, :]
    on_diag = tile_ids[:, None] == tile_ids[None, :]
    lower_part = jnp.where(strict, full_matrix, jnp.where(on_diag, 0.5 * full_matrix, 0.0))
    raw_panel = reflectors.reshape(matrix_order, TILE)
    within = jnp.arange(matrix_order, dtype=jnp.int32) % TILE
    column = jnp.arange(TILE, dtype=jnp.int32)
    unit_block = jnp.where(within[:, None] > column[None, :], raw_panel,
                           jnp.where(within[:, None] == column[None, :], 1.0, 0.0))
    vectors = jnp.where(tile_ids[:, None] == 0, 0.0, jnp.where(tile_ids[:, None] == 1, unit_block, raw_panel))
    image_all = jnp.dot(lower_part, vectors, precision=precise) + jnp.dot(lower_part.T, vectors, precision=precise)
    gram_total = jnp.dot(vectors.T, vectors, precision=precise)
    cross_total = jnp.dot(vectors.T, image_all, precision=precise)
    coefficient = invert_factor(gram_total)
    middle = jnp.dot(jnp.dot(coefficient.T, cross_total, precision=precise), coefficient, precision=precise)
    update_all = jnp.dot(image_all, coefficient, precision=precise) - 0.5 * jnp.dot(vectors, middle, precision=precise)

    def new_block(block_index):
        row_start = block_index * TILE
        rows_lower = lax.dynamic_slice_in_dim(lower_part, row_start, TILE, 0)
        cols_lower = lax.dynamic_slice_in_dim(lower_part, row_start, TILE, 1)
        symmetric = rows_lower + cols_lower.T
        update_rows = lax.dynamic_slice_in_dim(update_all, row_start, TILE, 0)
        vector_rows = lax.dynamic_slice_in_dim(vectors, row_start, TILE, 0)
        fresh = symmetric - jnp.dot(update_rows, vectors.T, precision=precise) - jnp.dot(vector_rows, update_all.T, precision=precise)
        keep_mask = block_index >= tile_ids[None, :]
        return jnp.where(keep_mask, fresh, 0.0)

    new_blocks = lax.map(new_block, jnp.arange(matrix_order // TILE, dtype=jnp.int32))
    return new_blocks.reshape(RT, N_PROW * TILE, CT, N_PCOL * TILE)
```

```python
import jax
import jax.numpy as jnp
from jax import lax
from jax.experimental import pallas as pl
from jax.experimental.pallas import tpu as pltpu
from jax.sharding import PartitionSpec as P

MESH = pl.DeviceIdType.MESH
f32 = jnp.float32
NP, NQ, T, S = 32, 16, 256, 16
Z = 16


def dot(a, b, ca=1, cb=0):
    return lax.dot_general(a, b, (((ca,), (cb,)), ((), ())), precision=lax.Precision.HIGHEST, preferred_element_type=f32)


def copy_to(src, dst, send_sem, recv_sem, p, q):
    return pltpu.make_async_remote_copy(
        src_ref=src, dst_ref=dst, send_sem=send_sem, recv_sem=recv_sem, device_id=(p, q), device_id_type=MESH
    )


def loop(lo, hi, fn):
    def step(i, carry):
        fn(i)
        return carry

    lax.fori_loop(lo, hi, step, 0)


def rows(ref, i, n=S):
    return ref.at[pl.ds(pl.multiple_of(i * n, n), n)]


def kernel(a_ref, r_ref, o_ref, vp, vc, low, pc, colbuf, accbuf, rowbuf, rpart, wsl, wp, wc, gfull, gs, gy, gz, gram,
           mpart, mswap, mh, mrs, ms, mz, mtot, stack, coef, yp, yc, gmat,
           v_s, v_r, c1_s, c1_r, c2_s, c2_r, row_s, row_r, wr_s, wr_r, wcol_s, wcol_r, gz_s, gz_r, ga_s, ga_r,
           sw_s, sw_r, mr_s, mr_r, mz_s, mz_r, ma_s, ma_r):
    p = lax.axis_index("prow")
    q = lax.axis_index("pcol")
    y = p // Z
    z = lax.rem(p, Z)
    core = lax.rem(q, 2)
    mate = q + 1 - 2 * core
    chip = y * 8 + q // 2
    far = (4, 8, 12)
    near = (15, 1, 2)
    last_q = jnp.minimum(p, NQ - 1)

    def plane_row(yy):
        return yy * Z + z

    def up(d):
        return y * Z + lax.rem(z + d, Z)

    barrier = pltpu.get_barrier_semaphore()

    def greet(pp, qq):
        pl.semaphore_signal(barrier, inc=1, device_id=(pp, qq), device_id_type=MESH)

    def greet_sources(j):
        for h in range(2):
            @pl.when(q + h * NQ < p)
            def _():
                greet(q + h * NQ, j)

    loop(0, NQ, greet_sources)
    loop(1, NP, lambda d: greet(lax.rem(p + d, NP), q))
    loop(1, NQ, lambda d: greet(p, lax.rem(q + d, NQ)))
    loop(0, 8, lambda i: greet(plane_row(1 - y), 2 * i + core))

    raw = r_ref[...]
    ii = lax.broadcasted_iota(jnp.int32, (T, T), 0)
    jj = lax.broadcasted_iota(jnp.int32, (T, T), 1)
    unit = jnp.where(ii > jj, raw, jnp.where(ii == jj, 1.0, 0.0))
    vec = jnp.where(p == 0, 0.0, jnp.where(p == 1, unit, raw))
    vp[...] = vec
    gfull[...] = dot(vec, vec, 0, 0)
    gs[0] = gfull[pl.ds(pl.multiple_of(q * S, S), S), :]
    for h in range(2):
        c = q + h * NQ

        @pl.when(c <= p)
        def _():
            tile = a_ref[:, h, :] * jnp.where(c < p, 1.0, 0.5)
            low[h] = tile
            pc[h] = dot(tile, vp[...], 0, 0)

        @pl.when(c == p)
        def _():
            vc[h] = vp[...]

    pl.semaphore_wait(barrier, (NP - 1 - p) + (NP - 1) + (NQ - 1) + 8)

    def v_copy(pp):
        return copy_to(rows(vp, q), rows(vc.at[y], q), v_s.at[pp], v_r.at[y], pp, z)

    loop(p + 1, NP, lambda pp: v_copy(pp).start())

    def gram_copy(k, stage, dst, pp):
        return copy_to(gs.at[stage], dst, gz_s.at[k], gz_r.at[k], pp, q)

    gy_copy = gram_copy(0, 0, gy, plane_row(1 - y))
    gy_copy.start()

    def c1_copy(h, j):
        return copy_to(rows(pc.at[h], j), colbuf.at[q + h * NQ], c1_s.at[h, j], c1_r.at[q + h * NQ], p, j)

    for h in range(2):
        @pl.when(q + h * NQ <= p)
        def _():
            def send(d):
                c1_copy(h, lax.rem(q + d, NQ)).start()

            loop(1, NQ, send)
            colbuf[q + h * NQ] = pc[h, pl.ds(pl.multiple_of(q * S, S), S), :]

    gy_copy.wait_recv()
    gs[1] = gs[0] + gy[...]
    g1 = [gram_copy(1 + k, 1, gz.at[k], up(d)) for k, d in enumerate(far)]
    for c in g1:
        c.start()

    def c2_copy(c):
        return copy_to(colbuf.at[c], accbuf.at[p], c2_s.at[c], c2_r.at[p], c, q)

    def c1_wait(c):
        @pl.when(lax.rem(c, NQ) != q)
        def _():
            copy_to(colbuf.at[c], colbuf.at[c], c1_s.at[0, 0], c1_r.at[c], p, q).wait_recv()

    def pass_on(c):
        c1_wait(c)
        c2_copy(c).start()

    loop(0, p, pass_on)
    c1_wait(p)

    for c in g1:
        c.wait_recv()
    gs[2] = (gs[1] + gz[0]) + (gz[1] + gz[2])
    g2 = [gram_copy(4 + k, 2, gz.at[3 + k], up(d)) for k, d in enumerate(near)]
    for c in g2:
        c.start()

    for h in range(2):
        @pl.when(q + h * NQ < p)
        def _():
            copy_to(vc.at[h], vc.at[h], v_s.at[0], v_r.at[h], p, q).wait_recv()

    @pl.when(q <= p)
    def _():
        rpart[...] = dot(low[0], vc[0])

    @pl.when(q + NQ <= p)
    def _():
        rpart[...] += dot(low[1], vc[1])

    def row_copy(j):
        return copy_to(rows(rpart, j), rowbuf.at[q], row_s.at[j], row_r.at[q], p, j)

    @pl.when(q <= p)
    def _():
        loop(1, NQ, lambda d: row_copy(lax.rem(q + d, NQ)).start())
        rowbuf[q] = rpart[pl.ds(pl.multiple_of(q * S, S), S), :]

    mpart[...] = jnp.zeros_like(mpart)
    for h in range(2):
        @pl.when(q + h * NQ <= p)
        def _():
            mpart[...] += dot(pc[h], vc[h], 0, 0)

    half = T // 2
    swap1 = copy_to(rows(mpart, 1 - core, half), mswap, sw_s.at[0], sw_r.at[0], p, mate)
    swap1.start()

    for c in g2:
        c.wait_recv()
    gs[3] = (gs[2] + gz[3]) + (gz[4] + gz[5])
    gram[pl.ds(pl.multiple_of(q * S, S), S), :] = gs[3]

    def gall_copy(j):
        return copy_to(gs.at[3], rows(gram, q), ga_s.at[j], ga_r.at[q], p, j)

    loop(1, NQ, lambda d: gall_copy(lax.rem(q + d, NQ)).start())

    swap1.wait_recv()
    mh[...] = mpart[pl.ds(pl.multiple_of(core * half, half), half), :] + mswap[...]

    def mr_copy(i):
        return copy_to(rows(mh, i, 8), mrs.at[chip], mr_s.at[i], mr_r.at[chip], plane_row(i // 8), 2 * lax.rem(i, 8) + core)

    loop(1, 16, lambda d: mr_copy(lax.rem(chip + d, 16)).start())
    mrs[chip] = mh[pl.ds(pl.multiple_of(chip * 8, 8), 8), :]

    wsl[...] = colbuf[p]

    def row_add(j):
        @pl.when(j != q)
        def _():
            copy_to(rowbuf.at[j], rowbuf.at[j], row_s.at[0], row_r.at[j], p, q).wait_recv()

        wsl[...] += rowbuf[j]

    def col_add(pp):
        copy_to(accbuf.at[pp], accbuf.at[pp], c2_s.at[0], c2_r.at[pp], p, q).wait_recv()
        wsl[...] += accbuf[pp]

    loop(0, last_q + 1, row_add)
    loop(p + 1, NP, col_add)

    def wcol_copy(pp):
        return copy_to(wsl, rows(wc.at[y], q), wcol_s.at[pp], wcol_r.at[y], pp, z)

    def wrow_copy(j):
        return copy_to(wsl, rows(wp, q), wr_s.at[j], wr_r.at[q], p, j)

    def not_me(j, fn):
        @pl.when(j != q)
        def _():
            fn(j)

    loop(p + 1, NP, lambda pp: wcol_copy(pp).start())
    loop(0, last_q + 1, lambda j: not_me(j, lambda i: wrow_copy(i).start()))
    wp[pl.ds(pl.multiple_of(q * S, S), S), :] = wsl[...]

    ms[0] = mrs[chip]

    def mr_add(d):
        i = lax.rem(chip + d, 16)
        copy_to(mrs.at[i], mrs.at[i], mr_s.at[0], mr_r.at[i], p, q).wait_recv()
        ms[0] += mrs[i]

    loop(1, 16, mr_add)

    def mz_copy(k, stage, pp):
        return copy_to(ms.at[stage], mz.at[k], mz_s.at[k], mz_r.at[k], pp, q)

    m1 = [mz_copy(k, 0, up(d)) for k, d in enumerate(far)]
    for c in m1:
        c.start()

    def gall_wait(d):
        j = lax.rem(q + d, NQ)
        copy_to(rows(gram, j), rows(gram, j), ga_s.at[0], ga_r.at[j], p, q).wait_recv()

    loop(1, NQ, gall_wait)
    diag = jnp.where(ii == jj, 0.5 * gram[...], 0.0)
    power = jnp.where(ii < jj, -gram[...], 0.0) / jnp.sum(diag, axis=1, keepdims=True)
    stack[0:T] = jnp.where(ii == jj, 1.0, power)
    stack[T:] = dot(power, power)

    def double(_):
        both = dot(stack[...], stack[T:])
        stack[0:T] += both[0:T]
        stack[T:] = both[T:]

    loop(0, 3, double)

    for c in m1:
        c.wait_recv()
    ms[1] = (ms[0] + mz[0]) + (mz[1] + mz[2])
    m2 = [mz_copy(3 + k, 1, up(d)) for k, d in enumerate(near)]
    for c in m2:
        c.start()

    loop(0, 3, double)
    coef[...] = (stack[0:T] + dot(stack[0:T], stack[T:])) / jnp.sum(diag, axis=0, keepdims=True)

    for c in m2:
        c.wait_recv()
    ms[2] = (ms[1] + mz[3]) + (mz[4] + mz[5])

    def place(i):
        return mtot.at[pl.ds(pl.multiple_of(core * half + i * 8, 8), 8)]

    def mall_copy(i):
        return copy_to(ms.at[2], place(chip), ma_s.at[i], ma_r.at[chip], plane_row(i // 8), 2 * lax.rem(i, 8) + core)

    loop(1, 16, lambda d: mall_copy(lax.rem(chip + d, 16)).start())
    mtot[pl.ds(pl.multiple_of(core * half + chip * 8, 8), 8), :] = ms[2]

    yp[...] = dot(vp[...], coef[...], 1, 1)
    for h in range(2):
        @pl.when(q + h * NQ <= p)
        def _():
            yc[h] = dot(vc[h], coef[...], 1, 1)

    def mall_wait(d):
        i = lax.rem(chip + d, 16)
        copy_to(place(i), place(i), ma_s.at[0], ma_r.at[i], p, q).wait_recv()

    loop(1, 16, mall_wait)
    swap2 = copy_to(rows(mtot, core, half), rows(mtot, core, half), sw_s.at[1], sw_r.at[1], p, mate)
    swap2.start()
    copy_to(rows(mtot, 1 - core, half), rows(mtot, 1 - core, half), sw_s.at[1], sw_r.at[1], p, mate).wait_recv()
    swap2.wait_send()
    cross = mtot[...] + mtot[...].T
    middle = dot(dot(coef[...], cross, 0, 0), coef[...])
    gmat[...] = dot(vp[...], middle)

    @pl.when(q <= p)
    def _():
        def wr_wait(j):
            copy_to(rows(wp, j), rows(wp, j), wr_s.at[0], wr_r.at[j], p, q).wait_recv()

        loop(0, NQ, lambda j: not_me(j, wr_wait))

    for h in range(2):
        c = q + h * NQ

        @pl.when(c < p)
        def _():
            copy_to(wc.at[h], wc.at[h], wcol_s.at[0], wcol_r.at[h], p, q).wait_recv()

        @pl.when(c == p)
        def _():
            wc[h] = wp[...]

        @pl.when(c <= p)
        def _():
            tile = a_ref[:, h, :]
            sym = jnp.where(c < p, tile, 0.5 * (tile + tile.T))
            o_ref[:, h, :] = (sym - dot(wp[...], yc[h], 1, 1) - dot(yp[...], wc[h], 1, 1)) + dot(gmat[...], vc[h], 1, 1)

        @pl.when(c > p)
        def _():
            o_ref[:, h, :] = jnp.zeros((T, T), f32)

    loop(p + 1, NP, lambda pp: v_copy(pp).wait_send())
    loop(p + 1, NP, lambda pp: wcol_copy(pp).wait_send())
    loop(0, p, lambda c: c2_copy(c).wait_send())
    for h in range(2):
        @pl.when(q + h * NQ <= p)
        def _():
            loop(1, NQ, lambda d: c1_copy(h, lax.rem(q + d, NQ)).wait_send())

    @pl.when(q <= p)
    def _():
        loop(1, NQ, lambda d: row_copy(lax.rem(q + d, NQ)).wait_send())

    loop(0, last_q + 1, lambda j: not_me(j, lambda i: wrow_copy(i).wait_send()))
    loop(1, NQ, lambda d: gall_copy(lax.rem(q + d, NQ)).wait_send())
    loop(1, 16, lambda d: mr_copy(lax.rem(chip + d, 16)).wait_send())
    loop(1, 16, lambda d: mall_copy(lax.rem(chip + d, 16)).wait_send())
    for c in [gy_copy, swap1] + g1 + g2 + m1 + m2:
        c.wait_send()


def body(matrix, reflectors):
    vmem = lambda *shape: pltpu.VMEM(shape, f32)
    dma = lambda *shape: pltpu.SemaphoreType.DMA(shape)
    out = pl.pallas_call(
        kernel,
        out_shape=jax.ShapeDtypeStruct((T, 2, T), f32),
        in_specs=[pl.BlockSpec(memory_space=pltpu.VMEM)] * 2,
        out_specs=pl.BlockSpec(memory_space=pltpu.VMEM),
        scratch_shapes=[
            vmem(T, T), vmem(2, T, T), vmem(2, T, T), vmem(2, T, T),
            vmem(NP, S, T), vmem(NP, S, T), vmem(NQ, S, T),
            vmem(T, T), vmem(S, T), vmem(T, T), vmem(2, T, T),
            vmem(T, T), vmem(4, S, T), vmem(S, T), vmem(6, S, T), vmem(T, T),
            vmem(T, T), vmem(T // 2, T), vmem(T // 2, T), vmem(16, 8, T), vmem(3, 8, T), vmem(6, 8, T), vmem(T, T),
            vmem(2 * T, T), vmem(T, T), vmem(T, T), vmem(2, T, T), vmem(T, T),
            dma(NP), dma(2), dma(2, NQ), dma(NP), dma(NP), dma(NP), dma(NQ), dma(NQ), dma(NQ), dma(NQ), dma(NP), dma(2),
            dma(7), dma(7), dma(NQ), dma(NQ),
            dma(2), dma(2), dma(16), dma(16), dma(6), dma(6), dma(16), dma(16),
        ],
        compiler_params=pltpu.CompilerParams(collective_id=0, has_side_effects=True, vmem_limit_bytes=40 * 2**20),
        cost_estimate=pl.CostEstimate(flops=34 * 2 * T**3, bytes_accessed=5 * T * T * 4, transcendentals=0),
    )(matrix.reshape(T, 2, T), reflectors.reshape(T, T))
    return out.reshape(matrix.shape)


def solution(mesh):
    placed = (P(None, "prow", None, "pcol"), P(None, "prow", None))
    return jax.shard_map(
        body, mesh=mesh, in_specs=placed, out_specs=P(None, "prow", None, "pcol"), check_vma=False
    )
```

```python
import jax
import jax.numpy as jnp
from jax import lax
from jax.experimental import pallas as pl
from jax.experimental.pallas import tpu as pltpu
from jax.sharding import PartitionSpec as P

MESH = pl.DeviceIdType.MESH
f32 = jnp.float32
NP, NQ, T, S = 32, 16, 256, 16
Z = 16
FAR = 5


def dot(a, b, ca=1, cb=0):
    return lax.dot_general(a, b, (((ca,), (cb,)), ((), ())), precision=lax.Precision.HIGHEST, preferred_element_type=f32)


def copy_to(src, dst, send_sem, recv_sem, p, q):
    return pltpu.make_async_remote_copy(
        src_ref=src, dst_ref=dst, send_sem=send_sem, recv_sem=recv_sem, device_id=(p, q), device_id_type=MESH
    )


def loop(lo, hi, fn):
    def step(i, carry):
        fn(i)
        return carry

    lax.fori_loop(lo, hi, step, 0)


def rows(ref, i, n=S):
    return ref.at[pl.ds(pl.multiple_of(i * n, n), n)]


def kernel(a_hbm, r_hbm, o_ref, a_ref, r_ref, vp, vc, low, pc, cbuf, abuf, rowbuf, rpart, wsl, wp, wc, vrel, wrel,
           gs, gx, gram, ms, mx, mtot, stack, coef, lhs, rhs,
           in_s, v_s, v_r, vf_s, vf_r, w_s, w_r, wf_s, wf_r, c1_s, c1_r, c2_s, c2_r, row_s, row_r, wr_s, wr_r,
           gx_s, gx_r, ga_s, ga_r, mx_s, mx_r, ma_s, ma_r):
    p = lax.axis_index("prow")
    q = lax.axis_index("pcol")
    y = p // Z
    z = lax.rem(p, Z)
    last_q = jnp.minimum(p, NQ - 1)
    get_r = pltpu.make_async_copy(r_hbm, r_ref, in_s.at[0])
    get_a = pltpu.make_async_copy(a_hbm, a_ref, in_s.at[1])
    get_r.start()
    get_a.start()

    def plane(d):
        return lax.rem(z + d + Z, Z)

    def not_me(j, fn):
        @pl.when(j != q)
        def _():
            fn(j)

    def source(k):
        return plane((0, -FAR, FAR)[k]), (5, 6, 5)[k]

    def targets(k, fn):
        t, n = source(k)

        def one(i):
            yy = lax.rem(i, 2)
            pp = yy * Z + plane(i // 2 - 2)
            fn(i, pp, t, pp > y * Z + t, (pp == p) & (t == q))

        loop(0, 2 * n, one)

    barrier = pltpu.get_barrier_semaphore()

    def greet(pp, qq):
        pl.semaphore_signal(barrier, inc=1, device_id=(pp, qq), device_id_type=MESH)

    off = lax.rem(z - q + 7 + Z, Z) - 7
    step = jnp.where(off < -2, -FAR, jnp.where(off > 2, FAR, 0))
    from_z = lax.rem(q + step + Z, Z)
    for h in range(2):
        @pl.when(q + h * NQ < p)
        def _():
            def hello(j):
                @pl.when((h != y) | (from_z != z) | (j != q))
                def _():
                    greet(h * Z + from_z, j)

            loop(0, NQ, hello)

    loop(1, Z, lambda d: greet(y * Z + plane(d), q))
    loop(1, 4, lambda d: greet((1 - y) * Z + plane(4 * d), q))
    loop(1, NQ, lambda d: greet(p, lax.rem(q + d, NQ)))
    loop(0, NQ, lambda j: greet((1 - y) * Z + z, j))
    count = jnp.int32(18 + 31)
    for k in range(3):
        t, n = source(k)
        for i in range(2 * n):
            pp = (i % 2) * Z + plane(i // 2 - 2)
            count += ((pp > y * Z + t) & ((pp != p) | (t != q))).astype(jnp.int32)

    get_r.wait()
    raw = r_ref[...]
    ii = lax.broadcasted_iota(jnp.int32, (T, T), 0)
    jj = lax.broadcasted_iota(jnp.int32, (T, T), 1)
    unit = jnp.where(ii > jj, raw, jnp.where(ii == jj, 1.0, 0.0))
    vp[...] = jnp.where(p == 0, 0.0, jnp.where(p == 1, unit, raw)).T
    gs[0] = dot(vp[pl.ds(pl.multiple_of(q * S, S), S), :], vp[...], 1, 1)
    get_a.wait()
    for h in range(2):
        c = q + h * NQ

        @pl.when(c <= p)
        def _():
            tile = a_ref[:, h, :] * jnp.where(c < p, 1.0, 0.5)
            low[h] = tile
            pc[h] = dot(vp[...], tile)

        @pl.when(c == p)
        def _():
            vc[h] = vp[...]

    pl.semaphore_wait(barrier, count)

    def first(src, rel, f_s, f_r):
        return [
            copy_to(src, rel.at[0], f_s.at[0], f_r.at[0], y * Z + plane(FAR), q),
            copy_to(src, rel.at[1], f_s.at[1], f_r.at[1], y * Z + plane(-FAR), q),
        ]

    def fan(k, src, dst, s_s, s_r):
        def send(i, pp, t, live, me):
            @pl.when(live & jnp.logical_not(me))
            def _():
                copy_to(src, rows(dst.at[y], q), s_s.at[k, i], s_r.at[y], pp, t).start()

            @pl.when(live & me)
            def _():
                pltpu.make_async_copy(src, rows(dst.at[y], q), s_r.at[y]).start()

        targets(k, send)

    def fan_done(k, src, dst, s_s, s_r):
        def done(i, pp, t, live, me):
            @pl.when(live & jnp.logical_not(me))
            def _():
                copy_to(src, rows(dst.at[y], q), s_s.at[k, i], s_r.at[y], pp, t).wait_send()

        targets(k, done)

    v_mine = rows(vp, q)
    v_first = first(v_mine, vrel, vf_s, vf_r)
    for c in v_first:
        c.start()
    fan(0, v_mine, vc, v_s, v_r)

    def c1_copy(h, j):
        return copy_to(rows(pc.at[h], j), cbuf.at[y, q], c1_s.at[h, j], c1_r.at[y, q], h * Z + z, j)

    def c1_each(h, fn):
        def one(d):
            j = lax.rem(q + d, NQ)

            @pl.when((h != y) | (j != q))
            def _():
                fn(c1_copy(h, j))

        loop(0, NQ, one)

    for h in range(2):
        @pl.when(q + h * NQ <= p)
        def _():
            c1_each(h, lambda c: c.start())

            @pl.when(h == y)
            def _():
                cbuf[y, q] = pc[h, pl.ds(pl.multiple_of(q * S, S), S), :]

    def sum_far(buf, got, s, r):
        out = []
        for k in range(7):
            d, other = (k + 1) // 2 * 4, (k + 1) % 2
            yy = 1 - y if other else y
            out.append(copy_to(buf.at[0], got.at[k], s.at[k], r.at[k], yy * Z + plane(d), q))
        return out

    def sum_near(buf, got, s, r):
        return [
            copy_to(buf.at[1], got.at[7 + k], s.at[7 + k], r.at[7 + k], y * Z + plane(d), q)
            for k, d in enumerate((-1, 1, 2))
        ]

    def sum_far_end(copies, buf, got):
        total = buf[0]
        for k, c in enumerate(copies):
            c.wait_recv()
            total += got[k]
        buf[1] = total

    def sum_near_end(copies, buf, got):
        total = buf[1]
        for k, c in enumerate(copies):
            c.wait_recv()
            total += got[7 + k]
        buf[2] = total

    def all_copy(buf, dst, s, r, j):
        return copy_to(buf.at[2], rows(dst, q), s.at[j], r.at[q], p, j)

    def all_send(buf, dst, s, r):
        loop(1, NQ, lambda d: all_copy(buf, dst, s, r, lax.rem(q + d, NQ)).start())
        dst[pl.ds(pl.multiple_of(q * S, S), S), :] = buf[2]

    def all_wait(dst, s, r):
        def one(j):
            copy_to(rows(dst, j), rows(dst, j), s.at[0], r.at[j], p, q).wait_recv()

        loop(0, NQ, lambda j: not_me(j, one))

    g_far = sum_far(gs, gx, gx_s, gx_r)
    for c in g_far:
        c.start()

    def relay(k, rel, f_s, f_r, dst, s_s, s_r):
        copy_to(rel.at[k - 1], rel.at[k - 1], f_s.at[k - 1], f_r.at[k - 1], p, q).wait_recv()
        fan(k, rel.at[k - 1], dst, s_s, s_r)

    for k in (1, 2):
        relay(k, vrel, vf_s, vf_r, vc, v_s, v_r)

    def c1_wait(yy, i):
        @pl.when((yy != y) | (i != q))
        def _():
            copy_to(cbuf.at[yy, i], cbuf.at[yy, i], c1_s.at[0, 0], c1_r.at[yy, i], p, q).wait_recv()

    def c2_copy(i):
        return copy_to(cbuf.at[1, i], abuf.at[z], c2_s.at[i], c2_r.at[z], y * Z + i, q)

    def c2_each(fn):
        def one(k):
            size = 8 - (k + 1) // 2
            i = plane(jnp.where(lax.rem(k, 2) == 1, size, -size))

            @pl.when((y == 0) | (i <= z))
            def _():
                fn(i)

        loop(0, Z, one)

    def c2_send(i):
        c1_wait(1, i)

        @pl.when((y == 0) & (i <= z))
        def _():
            c1_wait(0, i)
            cbuf[1, i] += cbuf[0, i]

        @pl.when(i != z)
        def _():
            c2_copy(i).start()

    c2_each(c2_send)

    sum_far_end(g_far, gs, gx)
    g_near = sum_near(gs, gx, gx_s, gx_r)
    for c in g_near:
        c.start()

    for h in range(2):
        @pl.when(q + h * NQ < p)
        def _():
            copy_to(vc.at[h], vc.at[h], v_s.at[0, 0], v_r.at[h], p, q).wait_recv()

    @pl.when(q <= p)
    def _():
        rpart[...] = dot(vc[0], low[0], 1, 1)

    @pl.when(q + NQ <= p)
    def _():
        rpart[...] += dot(vc[1], low[1], 1, 1)

    def row_copy(j):
        return copy_to(rows(rpart, j), rowbuf.at[q], row_s.at[j], row_r.at[q], p, j)

    @pl.when(q <= p)
    def _():
        loop(1, NQ, lambda d: row_copy(lax.rem(q + d, NQ)).start())
        rowbuf[q] = rpart[pl.ds(pl.multiple_of(q * S, S), S), :]

    sum_near_end(g_near, gs, gx)
    all_send(gs, gram, ga_s, ga_r)

    wsl[...] = cbuf[1, z]

    def col_add(i):
        @pl.when((i != z) & ((y == 0) | (i > z)))
        def _():
            copy_to(abuf.at[i], abuf.at[i], c2_s.at[0], c2_r.at[i], p, q).wait_recv()
            wsl[...] += abuf[i]

    loop(0, Z, col_add)
    ms[0] = dot(wsl[...], vp[...], 1, 1)
    m_far = sum_far(ms, mx, mx_s, mx_r)
    for c in m_far:
        c.start()

    def row_add(j):
        @pl.when(j != q)
        def _():
            copy_to(rowbuf.at[j], rowbuf.at[j], row_s.at[0], row_r.at[j], p, q).wait_recv()

        wsl[...] += rowbuf[j]

    loop(0, last_q + 1, row_add)
    w_first = first(wsl, wrel, wf_s, wf_r)
    for c in w_first:
        c.start()
    fan(0, wsl, wc, w_s, w_r)

    def wrow_copy(j):
        return copy_to(wsl, rows(wp, q), wr_s.at[j], wr_r.at[q], p, j)

    loop(0, last_q + 1, lambda j: not_me(j, lambda i: wrow_copy(i).start()))
    wp[pl.ds(pl.multiple_of(q * S, S), S), :] = wsl[...]

    all_wait(gram, ga_s, ga_r)
    diag = jnp.where(ii == jj, 0.5 * gram[...], 0.0)
    power = jnp.where(ii < jj, -gram[...], 0.0) / jnp.sum(diag, axis=1, keepdims=True)
    stack[0:T] = jnp.where(ii == jj, 1.0, power)
    stack[T:] = dot(power, power)

    def double(_):
        both = dot(stack[...], stack[T:])
        stack[0:T] += both[0:T]
        stack[T:] = both[T:]

    loop(0, 5, double)

    for k in (1, 2):
        relay(k, wrel, wf_s, wf_r, wc, w_s, w_r)

    sum_far_end(m_far, ms, mx)
    m_near = sum_near(ms, mx, mx_s, mx_r)
    for c in m_near:
        c.start()

    double(0)
    coef[...] = (stack[0:T] + dot(stack[0:T], stack[T:])) / jnp.sum(diag, axis=0, keepdims=True)

    sum_near_end(m_near, ms, mx)
    all_send(ms, mtot, ma_s, ma_r)
    lhs[T : 2 * T] = dot(coef[...], vp[...])
    for h in range(2):
        @pl.when(q + h * NQ <= p)
        def _():
            rhs[h, 0:T] = dot(coef[...], vc[h])
            rhs[h, 2 * T :] = vc[h]

    all_wait(mtot, ma_s, ma_r)
    cross = mtot[...] + mtot[...].T
    middle = dot(dot(coef[...], cross, 0, 0), coef[...])
    lhs[2 * T :] = dot(middle, vp[...])

    @pl.when(q <= p)
    def _():
        def wr_wait(j):
            copy_to(rows(wp, j), rows(wp, j), wr_s.at[0], wr_r.at[j], p, q).wait_recv()

        loop(0, NQ, lambda j: not_me(j, wr_wait))
        lhs[0:T] = -wp[...]
        lhs[T : 2 * T] = -lhs[T : 2 * T]

    for h in range(2):
        c = q + h * NQ

        @pl.when(c < p)
        def _():
            copy_to(wc.at[h], wc.at[h], w_s.at[0, 0], w_r.at[h], p, q).wait_recv()

        @pl.when(c == p)
        def _():
            wc[h] = wp[...]

        @pl.when(c <= p)
        def _():
            rhs[h, T : 2 * T] = wc[h]
            tile = a_ref[:, h, :]
            sym = jnp.where(c < p, tile, 0.5 * (tile + tile.T))
            o_ref[:, h, :] = sym + dot(lhs[...], rhs[h], 0, 0)

        @pl.when(c > p)
        def _():
            o_ref[:, h, :] = jnp.zeros((T, T), f32)

    for k, (v_src, w_src) in enumerate(((v_mine, wsl), (vrel.at[0], wrel.at[0]), (vrel.at[1], wrel.at[1]))):
        fan_done(k, v_src, vc, v_s, v_r)
        fan_done(k, w_src, wc, w_s, w_r)
    for h in range(2):
        @pl.when(q + h * NQ <= p)
        def _():
            c1_each(h, lambda c: c.wait_send())

    def c2_sent(i):
        @pl.when(i != z)
        def _():
            c2_copy(i).wait_send()

    c2_each(c2_sent)

    @pl.when(q <= p)
    def _():
        loop(1, NQ, lambda d: row_copy(lax.rem(q + d, NQ)).wait_send())

    loop(0, last_q + 1, lambda j: not_me(j, lambda i: wrow_copy(i).wait_send()))
    loop(1, NQ, lambda d: all_copy(gs, gram, ga_s, ga_r, lax.rem(q + d, NQ)).wait_send())
    loop(1, NQ, lambda d: all_copy(ms, mtot, ma_s, ma_r, lax.rem(q + d, NQ)).wait_send())
    for c in v_first + w_first + g_far + g_near + m_far + m_near:
        c.wait_send()


def body(matrix, reflectors):
    vmem = lambda *shape: pltpu.VMEM(shape, f32)
    dma = lambda *shape: pltpu.SemaphoreType.DMA(shape)
    out = pl.pallas_call(
        kernel,
        out_shape=jax.ShapeDtypeStruct((T, 2, T), f32),
        in_specs=[pl.BlockSpec(memory_space=pltpu.HBM)] * 2,
        out_specs=pl.BlockSpec(memory_space=pltpu.VMEM),
        scratch_shapes=[
            vmem(T, 2, T), vmem(T, T),
            vmem(T, T), vmem(2, T, T), vmem(2, T, T), vmem(2, T, T),
            vmem(2, NQ, S, T), vmem(Z, S, T), vmem(NQ, S, T),
            vmem(T, T), vmem(S, T), vmem(T, T), vmem(2, T, T), vmem(2, S, T), vmem(2, S, T),
            vmem(3, S, T), vmem(10, S, T), vmem(T, T), vmem(3, S, T), vmem(10, S, T), vmem(T, T),
            vmem(2 * T, T), vmem(T, T), vmem(3 * T, T), vmem(2, 3 * T, T),
            dma(2), dma(3, 12), dma(2), dma(2), dma(2), dma(3, 12), dma(2), dma(2), dma(2),
            dma(2, NQ), dma(2, NQ), dma(Z), dma(Z), dma(NQ), dma(NQ), dma(NQ), dma(NQ),
            dma(10), dma(10), dma(NQ), dma(NQ), dma(10), dma(10), dma(NQ), dma(NQ),
        ],
        compiler_params=pltpu.CompilerParams(collective_id=0, has_side_effects=True, vmem_limit_bytes=40 * 2**20),
        cost_estimate=pl.CostEstimate(flops=34 * 2 * T**3, bytes_accessed=5 * T * T * 4, transcendentals=0),
    )(matrix.reshape(T, 2, T), reflectors.reshape(T, T))
    return out.reshape(matrix.shape)


def solution(mesh):
    placed = (P(None, "prow", None, "pcol"), P(None, "prow", None))
    return jax.shard_map(
        body, mesh=mesh, in_specs=placed, out_specs=P(None, "prow", None, "pcol"), check_vma=False
    )
```

```python
import jax
import jax.numpy as jnp
from jax import lax
from jax.experimental import pallas as pl
from jax.experimental.pallas import tpu as pltpu
from jax.sharding import PartitionSpec as P

MESH = pl.DeviceIdType.MESH
f32 = jnp.float32
NP, NQ, T, S = 32, 16, 256, 16
Z = 16
FAR = 5


def dot(a, b, ca=1, cb=0):
    return lax.dot_general(a, b, (((ca,), (cb,)), ((), ())), precision=lax.Precision.HIGHEST, preferred_element_type=f32)


def copy_to(src, dst, send_sem, recv_sem, p, q):
    return pltpu.make_async_remote_copy(
        src_ref=src, dst_ref=dst, send_sem=send_sem, recv_sem=recv_sem, device_id=(p, q), device_id_type=MESH
    )


def loop(lo, hi, fn):
    def step(i, carry):
        fn(i)
        return carry

    lax.fori_loop(lo, hi, step, 0)


def rows(ref, i, n=S):
    return ref.at[pl.ds(pl.multiple_of(i * n, n), n)]


def kernel(a_hbm, r_hbm, o_ref, a_ref, r_ref, vp, vc, low, pc, cbuf, nbuf, psum, abuf, rowbuf, rpart, wsl, wp, wc, vrel, wrel,
           gs, gx, gram, ms, mx, mtot, stack, coef, lhs, rhs,
           in_s, v_s, v_r, vf_s, vf_r, w_s, w_r, wf_s, wf_r, c1_s, c1_r, c2_s, c2_r, c3_s, c3_r, row_s, row_r, wr_s, wr_r,
           gx_s, gx_r, ga_s, ga_r, mx_s, mx_r, ma_s, ma_r):
    p = lax.axis_index("prow")
    q = lax.axis_index("pcol")
    y = p // Z
    z = lax.rem(p, Z)
    last_q = jnp.minimum(p, NQ - 1)
    get_r = pltpu.make_async_copy(r_hbm, r_ref, in_s.at[0])
    get_a = pltpu.make_async_copy(a_hbm, a_ref, in_s.at[1])
    get_r.start()
    get_a.start()

    def plane(d):
        return lax.rem(z + d + Z, Z)

    def not_me(j, fn):
        @pl.when(j != q)
        def _():
            fn(j)

    def source(k):
        return plane((0, -FAR, FAR)[k]), (5, 6, 5)[k]

    def targets(k, fn):
        t, n = source(k)

        def one(i):
            yy = lax.rem(i, 2)
            pp = yy * Z + plane(i // 2 - 2)
            fn(i, pp, t, pp > y * Z + t, (pp == p) & (t == q))

        loop(0, 2 * n, one)

    barrier = pltpu.get_barrier_semaphore()

    def greet(pp, qq):
        pl.semaphore_signal(barrier, inc=1, device_id=(pp, qq), device_id_type=MESH)

    off = lax.rem(z - q + 7 + Z, Z) - 7
    step = jnp.where(off < -2, -FAR, jnp.where(off > 2, FAR, 0))
    from_z = lax.rem(q + step + Z, Z)
    for h in range(2):
        @pl.when(q + h * NQ < p)
        def _():
            def hello(j):
                @pl.when((h != y) | (from_z != z) | (j != q))
                def _():
                    greet(h * Z + from_z, j)

            loop(0, NQ, hello)

    loop(1, Z, lambda d: greet(y * Z + plane(d), q))
    loop(1, 4, lambda d: greet((1 - y) * Z + plane(4 * d), q))
    loop(1, NQ, lambda d: greet(p, lax.rem(q + d, NQ)))
    loop(0, NQ, lambda j: greet((1 - y) * Z + z, j))
    count = jnp.int32(18 + 31)
    for k in range(3):
        t, n = source(k)
        for i in range(2 * n):
            pp = (i % 2) * Z + plane(i // 2 - 2)
            count += ((pp > y * Z + t) & ((pp != p) | (t != q))).astype(jnp.int32)

    get_r.wait()
    raw = r_ref[...]
    ii = lax.broadcasted_iota(jnp.int32, (T, T), 0)
    jj = lax.broadcasted_iota(jnp.int32, (T, T), 1)
    unit = jnp.where(ii > jj, raw, jnp.where(ii == jj, 1.0, 0.0))
    vp[...] = jnp.where(p == 0, 0.0, jnp.where(p == 1, unit, raw)).T
    gs[0] = dot(vp[pl.ds(pl.multiple_of(q * S, S), S), :], vp[...], 1, 1)
    get_a.wait()
    for h in range(2):
        c = q + h * NQ

        @pl.when(c <= p)
        def _():
            tile = a_ref[:, h, :] * jnp.where(c < p, 1.0, 0.5)
            low[h] = tile
            pc[h] = dot(vp[...], tile)

        @pl.when(c == p)
        def _():
            vc[h] = vp[...]

    pl.semaphore_wait(barrier, count)

    def first(src, rel, f_s, f_r):
        return [
            copy_to(src, rel.at[0], f_s.at[0], f_r.at[0], y * Z + plane(FAR), q),
            copy_to(src, rel.at[1], f_s.at[1], f_r.at[1], y * Z + plane(-FAR), q),
        ]

    def fan(k, src, dst, s_s, s_r):
        def send(i, pp, t, live, me):
            @pl.when(live & jnp.logical_not(me))
            def _():
                copy_to(src, rows(dst.at[y], q), s_s.at[k, i], s_r.at[y], pp, t).start()

            @pl.when(live & me)
            def _():
                pltpu.make_async_copy(src, rows(dst.at[y], q), s_r.at[y]).start()

        targets(k, send)

    def fan_done(k, src, dst, s_s, s_r):
        def done(i, pp, t, live, me):
            @pl.when(live & jnp.logical_not(me))
            def _():
                copy_to(src, rows(dst.at[y], q), s_s.at[k, i], s_r.at[y], pp, t).wait_send()

        targets(k, done)

    v_mine = rows(vp, q)
    v_first = first(v_mine, vrel, vf_s, vf_r)
    for c in v_first:
        c.start()

    def c1_copy(h, j):
        return copy_to(rows(pc.at[h], j), cbuf.at[y, q], c1_s.at[h, j], c1_r.at[y, q], h * Z + z, j)

    def c1_each(h, fn):
        def one(d):
            j = lax.rem(q + d, NQ)

            @pl.when((h != y) | (j != q))
            def _():
                fn(c1_copy(h, j))

        loop(0, NQ, one)

    for h in range(2):
        @pl.when(q + h * NQ <= p)
        def _():
            c1_each(h, lambda c: c.start())

            @pl.when(h == y)
            def _():
                cbuf[y, q] = pc[h, pl.ds(pl.multiple_of(q * S, S), S), :]

    fan(0, v_mine, vc, v_s, v_r)

    def sum_far(buf, got, s, r):
        out = []
        for k in range(7):
            d, other = (k + 1) // 2 * 4, (k + 1) % 2
            yy = 1 - y if other else y
            out.append(copy_to(buf.at[0], got.at[k], s.at[k], r.at[k], yy * Z + plane(d), q))
        return out

    def sum_near(buf, got, s, r):
        return [
            copy_to(buf.at[1], got.at[7 + k], s.at[7 + k], r.at[7 + k], y * Z + plane(d), q)
            for k, d in enumerate((-1, 1, 2))
        ]

    def sum_far_end(copies, buf, got):
        total = buf[0]
        for k, c in enumerate(copies):
            c.wait_recv()
            total += got[k]
        buf[1] = total

    def sum_near_end(copies, buf, got):
        total = buf[1]
        for k, c in enumerate(copies):
            c.wait_recv()
            total += got[7 + k]
        buf[2] = total

    def all_copy(buf, dst, s, r, j):
        return copy_to(buf.at[2], rows(dst, q), s.at[j], r.at[q], p, j)

    def all_send(buf, dst, s, r):
        loop(1, NQ, lambda d: all_copy(buf, dst, s, r, lax.rem(q + d, NQ)).start())
        dst[pl.ds(pl.multiple_of(q * S, S), S), :] = buf[2]

    def all_wait(dst, s, r):
        def one(j):
            copy_to(rows(dst, j), rows(dst, j), s.at[0], r.at[j], p, q).wait_recv()

        loop(0, NQ, lambda j: not_me(j, one))

    g_far = sum_far(gs, gx, gx_s, gx_r)
    for c in g_far:
        c.start()

    def relay(k, rel, f_s, f_r, dst, s_s, s_r):
        copy_to(rel.at[k - 1], rel.at[k - 1], f_s.at[k - 1], f_r.at[k - 1], p, q).wait_recv()
        fan(k, rel.at[k - 1], dst, s_s, s_r)

    for k in (1, 2):
        relay(k, vrel, vf_s, vf_r, vc, v_s, v_r)

    def c1_wait(yy, i):
        @pl.when((yy != y) | (i != q))
        def _():
            copy_to(cbuf.at[yy, i], cbuf.at[yy, i], c1_s.at[0, 0], c1_r.at[yy, i], p, q).wait_recv()

    def group(n):
        off = n - 7
        k = jnp.where(off > 2, 1, jnp.where(off < -2, 2, 0))
        a = jnp.where(off > 2, FAR, jnp.where(off < -2, -FAR, 0))
        return plane(-off), k, a, off - a

    def c2_copy(n):
        i, k, a, b = group(n)
        return copy_to(cbuf.at[1, i], nbuf.at[k, b + 2], c2_s.at[n], c2_r.at[k, b + 2], y * Z + plane(-b), q)

    def c2_each(fn):
        def one(n):
            i, k, a, b = group(n)

            @pl.when((y == 0) | (i <= z))
            def _():
                fn(n, i, b)

        loop(0, Z, one)

    def c2_send(n, i, b):
        c1_wait(1, i)

        @pl.when((y == 0) & (i <= z))
        def _():
            c1_wait(0, i)
            cbuf[1, i] += cbuf[0, i]

        @pl.when(b != 0)
        def _():
            c2_copy(n).start()

    c2_each(c2_send)

    def c3_copy(k):
        return copy_to(psum.at[k], abuf.at[k - 1], c3_s.at[k - 1], c3_r.at[k - 1], y * Z + source(k)[0], q)

    def c3_sum(k):
        t, n = source(k)
        psum[k] = jnp.zeros((S, T), f32)

        @pl.when((y == 0) | (t <= z))
        def _():
            psum[k] = cbuf[1, t]

        def add(i):
            @pl.when((i != 2) & ((y == 0) | (t <= plane(i - 2))))
            def _():
                copy_to(nbuf.at[k, i], nbuf.at[k, i], c2_s.at[0], c2_r.at[k, i], p, q).wait_recv()
                psum[k] += nbuf[k, i]

        loop(0, n, add)


    sum_far_end(g_far, gs, gx)
    g_near = sum_near(gs, gx, gx_s, gx_r)
    for c in g_near:
        c.start()

    for k in (1, 2):
        c3_sum(k)
        c3_copy(k).start()
    c3_sum(0)

    for h in range(2):
        @pl.when(q + h * NQ < p)
        def _():
            copy_to(vc.at[h], vc.at[h], v_s.at[0, 0], v_r.at[h], p, q).wait_recv()

    @pl.when(q <= p)
    def _():
        rpart[...] = dot(vc[0], low[0], 1, 1)

    @pl.when(q + NQ <= p)
    def _():
        rpart[...] += dot(vc[1], low[1], 1, 1)

    def row_copy(j):
        return copy_to(rows(rpart, j), rowbuf.at[q], row_s.at[j], row_r.at[q], p, j)

    @pl.when(q <= p)
    def _():
        loop(1, NQ, lambda d: row_copy(lax.rem(q + d, NQ)).start())
        rowbuf[q] = rpart[pl.ds(pl.multiple_of(q * S, S), S), :]

    sum_near_end(g_near, gs, gx)
    all_send(gs, gram, ga_s, ga_r)

    wsl[...] = psum[0]
    for k in (1, 2):
        copy_to(abuf.at[k - 1], abuf.at[k - 1], c3_s.at[0], c3_r.at[k - 1], p, q).wait_recv()
        wsl[...] += abuf[k - 1]
    ms[0] = dot(wsl[...], vp[...], 1, 1)
    m_far = sum_far(ms, mx, mx_s, mx_r)
    for c in m_far:
        c.start()

    def row_add(j):
        @pl.when(j != q)
        def _():
            copy_to(rowbuf.at[j], rowbuf.at[j], row_s.at[0], row_r.at[j], p, q).wait_recv()

        wsl[...] += rowbuf[j]

    loop(0, last_q + 1, row_add)
    w_first = first(wsl, wrel, wf_s, wf_r)
    for c in w_first:
        c.start()
    fan(0, wsl, wc, w_s, w_r)

    def wrow_copy(j):
        return copy_to(wsl, rows(wp, q), wr_s.at[j], wr_r.at[q], p, j)

    loop(0, last_q + 1, lambda j: not_me(j, lambda i: wrow_copy(i).start()))
    wp[pl.ds(pl.multiple_of(q * S, S), S), :] = wsl[...]

    all_wait(gram, ga_s, ga_r)
    diag = jnp.where(ii == jj, 0.5 * gram[...], 0.0)
    power = jnp.where(ii < jj, -gram[...], 0.0) / jnp.sum(diag, axis=1, keepdims=True)
    stack[0:T] = jnp.where(ii == jj, 1.0, power)
    stack[T:] = dot(power, power)

    def double(_):
        both = dot(stack[...], stack[T:])
        stack[0:T] += both[0:T]
        stack[T:] = both[T:]

    loop(0, 4, double)

    sum_far_end(m_far, ms, mx)
    m_near = sum_near(ms, mx, mx_s, mx_r)
    for c in m_near:
        c.start()

    for k in (1, 2):
        relay(k, wrel, wf_s, wf_r, wc, w_s, w_r)

    loop(0, 2, double)
    coef[...] = (stack[0:T] + dot(stack[0:T], stack[T:])) / jnp.sum(diag, axis=0, keepdims=True)

    sum_near_end(m_near, ms, mx)
    all_send(ms, mtot, ma_s, ma_r)
    lhs[T : 2 * T] = dot(coef[...], vp[...])
    for h in range(2):
        @pl.when(q + h * NQ <= p)
        def _():
            rhs[h, 0:T] = dot(coef[...], vc[h])
            rhs[h, 2 * T :] = vc[h]

    all_wait(mtot, ma_s, ma_r)
    cross = mtot[...] + mtot[...].T
    middle = dot(dot(coef[...], cross, 0, 0), coef[...])
    lhs[2 * T :] = dot(middle, vp[...])

    @pl.when(q <= p)
    def _():
        def wr_wait(j):
            copy_to(rows(wp, j), rows(wp, j), wr_s.at[0], wr_r.at[j], p, q).wait_recv()

        loop(0, NQ, lambda j: not_me(j, wr_wait))
        lhs[0:T] = -wp[...]
        lhs[T : 2 * T] = -lhs[T : 2 * T]

    for h in range(2):
        c = q + h * NQ

        @pl.when(c < p)
        def _():
            copy_to(wc.at[h], wc.at[h], w_s.at[0, 0], w_r.at[h], p, q).wait_recv()

        @pl.when(c == p)
        def _():
            wc[h] = wp[...]

        @pl.when(c <= p)
        def _():
            rhs[h, T : 2 * T] = wc[h]
            tile = a_ref[:, h, :]
            sym = jnp.where(c < p, tile, 0.5 * (tile + tile.T))
            o_ref[:, h, :] = sym + dot(lhs[...], rhs[h], 0, 0)

        @pl.when(c > p)
        def _():
            o_ref[:, h, :] = jnp.zeros((T, T), f32)

    for k, (v_src, w_src) in enumerate(((v_mine, wsl), (vrel.at[0], wrel.at[0]), (vrel.at[1], wrel.at[1]))):
        fan_done(k, v_src, vc, v_s, v_r)
        fan_done(k, w_src, wc, w_s, w_r)
    for h in range(2):
        @pl.when(q + h * NQ <= p)
        def _():
            c1_each(h, lambda c: c.wait_send())

    def c2_sent(n, i, b):
        @pl.when(b != 0)
        def _():
            c2_copy(n).wait_send()

    c2_each(c2_sent)
    for k in (1, 2):
        c3_copy(k).wait_send()

    @pl.when(q <= p)
    def _():
        loop(1, NQ, lambda d: row_copy(lax.rem(q + d, NQ)).wait_send())

    loop(0, last_q + 1, lambda j: not_me(j, lambda i: wrow_copy(i).wait_send()))
    loop(1, NQ, lambda d: all_copy(gs, gram, ga_s, ga_r, lax.rem(q + d, NQ)).wait_send())
    loop(1, NQ, lambda d: all_copy(ms, mtot, ma_s, ma_r, lax.rem(q + d, NQ)).wait_send())
    for c in v_first + w_first + g_far + g_near + m_far + m_near:
        c.wait_send()


def body(matrix, reflectors):
    vmem = lambda *shape: pltpu.VMEM(shape, f32)
    dma = lambda *shape: pltpu.SemaphoreType.DMA(shape)
    out = pl.pallas_call(
        kernel,
        out_shape=jax.ShapeDtypeStruct((T, 2, T), f32),
        in_specs=[pl.BlockSpec(memory_space=pltpu.HBM)] * 2,
        out_specs=pl.BlockSpec(memory_space=pltpu.VMEM),
        scratch_shapes=[
            vmem(T, 2, T), vmem(T, T),
            vmem(T, T), vmem(2, T, T), vmem(2, T, T), vmem(2, T, T),
            vmem(2, NQ, S, T), vmem(3, 6, S, T), vmem(3, S, T), vmem(2, S, T), vmem(NQ, S, T),
            vmem(T, T), vmem(S, T), vmem(T, T), vmem(2, T, T), vmem(2, S, T), vmem(2, S, T),
            vmem(3, S, T), vmem(10, S, T), vmem(T, T), vmem(3, S, T), vmem(10, S, T), vmem(T, T),
            vmem(2 * T, T), vmem(T, T), vmem(3 * T, T), vmem(2, 3 * T, T),
            dma(2), dma(3, 12), dma(2), dma(2), dma(2), dma(3, 12), dma(2), dma(2), dma(2),
            dma(2, NQ), dma(2, NQ), dma(Z), dma(3, 6), dma(2), dma(2), dma(NQ), dma(NQ), dma(NQ), dma(NQ),
            dma(10), dma(10), dma(NQ), dma(NQ), dma(10), dma(10), dma(NQ), dma(NQ),
        ],
        compiler_params=pltpu.CompilerParams(collective_id=0, has_side_effects=True, vmem_limit_bytes=60 * 2**20),
        cost_estimate=pl.CostEstimate(flops=34 * 2 * T**3, bytes_accessed=5 * T * T * 4, transcendentals=0),
    )(matrix.reshape(T, 2, T), reflectors.reshape(T, T))
    return out.reshape(matrix.shape)


def solution(mesh):
    placed = (P(None, "prow", None, "pcol"), P(None, "prow", None))
    return jax.shard_map(
        body, mesh=mesh, in_specs=placed, out_specs=P(None, "prow", None, "pcol"), check_vma=False
    )
```

```python
import jax
import jax.numpy as jnp
from jax import lax
from jax.experimental import pallas as pl
from jax.experimental.pallas import tpu as pltpu
from jax.sharding import PartitionSpec as P

MESH = pl.DeviceIdType.MESH
f32 = jnp.float32
NP, NQ, T, S = 32, 16, 256, 16
Z = 16
FAR = 5


def dot(a, b, ca=1, cb=0):
    return lax.dot_general(a, b, (((ca,), (cb,)), ((), ())), precision=lax.Precision.HIGHEST, preferred_element_type=f32)


def copy_to(src, dst, send_sem, recv_sem, p, q):
    return pltpu.make_async_remote_copy(
        src_ref=src, dst_ref=dst, send_sem=send_sem, recv_sem=recv_sem, device_id=(p, q), device_id_type=MESH
    )


def loop(lo, hi, fn):
    def step(i, carry):
        fn(i)
        return carry

    lax.fori_loop(lo, hi, step, 0)


def rows(ref, i, n=S):
    return ref.at[pl.ds(pl.multiple_of(i * n, n), n)]


def kernel(a_hbm, r_hbm, o_ref, a_ref, r_ref, vp, vc, low, pc, cbuf, nbuf, psum, abuf, rowbuf, rpart, wsl, wp, vrel, wrel,
           gs, gx, gram, ms, mx, mtot, stack, coef, yp, lhs, rhs,
           in_s, v_s, v_r, vf_s, vf_r, w_s, w_r, wf_s, wf_r, c1_s, c1_r, c2_s, c2_r, c3_s, c3_r, row_s, row_r, wr_s, wr_r,
           gx_s, gx_r, ga_s, ga_r, mx_s, mx_r, ma_s, ma_r):
    p = lax.axis_index("prow")
    q = lax.axis_index("pcol")
    y = p // Z
    z = lax.rem(p, Z)
    last_q = jnp.minimum(p, NQ - 1)
    get_r = pltpu.make_async_copy(r_hbm, r_ref, in_s.at[0])
    get_a = pltpu.make_async_copy(a_hbm, a_ref, in_s.at[1])
    get_r.start()
    get_a.start()

    def plane(d):
        return lax.rem(z + d + Z, Z)

    def not_me(j, fn):
        @pl.when(j != q)
        def _():
            fn(j)

    def source(k):
        return plane((0, -FAR, FAR)[k]), (5, 6, 5)[k]

    def targets(k, fn):
        t, n = source(k)

        def one(i):
            yy = lax.rem(i, 2)
            pp = yy * Z + plane(i // 2 - 2)
            fn(i, pp, t, pp > y * Z + t, (pp == p) & (t == q))

        loop(0, 2 * n, one)

    barrier = pltpu.get_barrier_semaphore()

    def greet(pp, qq):
        pl.semaphore_signal(barrier, inc=1, device_id=(pp, qq), device_id_type=MESH)

    for d in (8, FAR, -FAR):
        greet((1 - y) * Z + plane(d), q)
    loop(1, Z, lambda d: greet(y * Z + plane(d), q))
    off = lax.rem(z - q + 7 + Z, Z) - 7
    step = jnp.where(off < -2, -FAR, jnp.where(off > 2, FAR, 0))
    from_z = lax.rem(q + step + Z, Z)
    for h in range(2):
        @pl.when(q + h * NQ < p)
        def _():
            def hello(j):
                @pl.when((h != y) | (from_z != z) | (j != q))
                def _():
                    greet(h * Z + from_z, j)

            loop(0, NQ, hello)

    loop(1, NQ, lambda d: greet(p, lax.rem(q + d, NQ)))
    loop(0, NQ, lambda j: greet((1 - y) * Z + z, j))
    count = jnp.int32(18 + 31)
    for k in range(3):
        t, n = source(k)
        for i in range(2 * n):
            pp = (i % 2) * Z + plane(i // 2 - 2)
            count += ((pp > y * Z + t) & ((pp != p) | (t != q))).astype(jnp.int32)

    get_r.wait()
    raw = r_ref[...]
    ii = lax.broadcasted_iota(jnp.int32, (T, T), 0)
    jj = lax.broadcasted_iota(jnp.int32, (T, T), 1)
    unit = jnp.where(ii > jj, raw, jnp.where(ii == jj, 1.0, 0.0))
    vp[...] = jnp.where(p == 0, 0.0, jnp.where(p == 1, unit, raw)).T
    gs[0] = dot(vp[pl.ds(pl.multiple_of(q * S, S), S), :], vp[...], 1, 1)
    get_a.wait()
    for h in range(2):
        c = q + h * NQ

        @pl.when(c <= p)
        def _():
            tile = a_ref[:, h, :] * jnp.where(c < p, 1.0, 0.5)
            low[h] = tile
            pc[h] = dot(vp[...], tile)

        @pl.when(c == p)
        def _():
            vc[h] = vp[...]

    pl.semaphore_wait(barrier, count)

    def first(src, rel, f_s, f_r):
        return [
            copy_to(src, rel.at[0], f_s.at[0], f_r.at[0], y * Z + plane(FAR), q),
            copy_to(src, rel.at[1], f_s.at[1], f_r.at[1], y * Z + plane(-FAR), q),
        ]

    def fan(k, src, dst, s_s, s_r):
        def send(i, pp, t, live, me):
            @pl.when(live & jnp.logical_not(me))
            def _():
                copy_to(src, dst, s_s.at[k, i], s_r.at[y], pp, t).start()

            @pl.when(live & me)
            def _():
                pltpu.make_async_copy(src, dst, s_r.at[y]).start()

        targets(k, send)

    def fan_done(k, src, dst, s_s, s_r):
        def done(i, pp, t, live, me):
            @pl.when(live & jnp.logical_not(me))
            def _():
                copy_to(src, dst, s_s.at[k, i], s_r.at[y], pp, t).wait_send()

        targets(k, done)

    v_mine = rows(vp, q)
    v_dst = rows(vc.at[y], q)
    w_dst = rhs.at[y, pl.ds(pl.multiple_of(T + q * S, S), S)]
    v_first = first(v_mine, vrel, vf_s, vf_r)
    for c in v_first:
        c.start()
    fan(0, v_mine, v_dst, v_s, v_r)

    def c1_copy(h, j):
        return copy_to(rows(pc.at[h], j), cbuf.at[y, q], c1_s.at[h, j], c1_r.at[y, q], h * Z + z, j)

    def c1_each(h, fn):
        def one(d):
            j = lax.rem(q + d, NQ)

            @pl.when((h != y) | (j != q))
            def _():
                fn(c1_copy(h, j))

        loop(0, NQ, one)

    for h in range(2):
        @pl.when(q + h * NQ <= p)
        def _():
            c1_each(h, lambda c: c.start())

            @pl.when(h == y)
            def _():
                cbuf[y, q] = pc[h, pl.ds(pl.multiple_of(q * S, S), S), :]


    def sum_far(buf, got, s, r):
        out = []
        for k, (d, other) in enumerate(((8, 0), (8, 1), (FAR, 0), (-FAR, 0), (FAR, 1), (-FAR, 1), (0, 1))):
            yy = 1 - y if other else y
            out.append(copy_to(buf.at[0], got.at[k], s.at[k], r.at[k], yy * Z + plane(d), q))
        return out

    def sum_near(buf, got, s, r):
        return [
            copy_to(buf.at[1], got.at[7 + k], s.at[7 + k], r.at[7 + k], y * Z + plane(d), q)
            for k, d in enumerate((-2, 2, -1, 1))
        ]

    def sum_far_end(copies, buf, got):
        total = buf[0]
        for k in range(2, 7):
            copies[k].wait_recv()
            total += got[k]
        buf[1] = total

    def sum_near_end(far, near, buf, got):
        total = buf[1]
        for k, c in enumerate(far[:2] + near):
            c.wait_recv()
            total += got[k if k < 2 else k + 5]
        buf[2] = total

    def all_copy(buf, dst, s, r, j):
        return copy_to(buf.at[2], rows(dst, q), s.at[j], r.at[q], p, j)

    def all_send(buf, dst, s, r):
        loop(1, NQ, lambda d: all_copy(buf, dst, s, r, lax.rem(q + d, NQ)).start())
        dst[pl.ds(pl.multiple_of(q * S, S), S), :] = buf[2]

    def all_wait(dst, s, r):
        def one(j):
            copy_to(rows(dst, j), rows(dst, j), s.at[0], r.at[j], p, q).wait_recv()

        loop(0, NQ, lambda j: not_me(j, one))

    g_far = sum_far(gs, gx, gx_s, gx_r)
    for c in g_far:
        c.start()

    def relay(k, rel, f_s, f_r, dst, s_s, s_r):
        copy_to(rel.at[k - 1], rel.at[k - 1], f_s.at[k - 1], f_r.at[k - 1], p, q).wait_recv()
        fan(k, rel.at[k - 1], dst, s_s, s_r)

    for k in (1, 2):
        relay(k, vrel, vf_s, vf_r, v_dst, v_s, v_r)

    def c1_wait(yy, i):
        @pl.when((yy != y) | (i != q))
        def _():
            copy_to(cbuf.at[yy, i], cbuf.at[yy, i], c1_s.at[0, 0], c1_r.at[yy, i], p, q).wait_recv()

    def group(n):
        off = jnp.where(n < 6, n + 3, jnp.where(n < 11, 3 - n, n - 13))
        k = jnp.where(off > 2, 1, jnp.where(off < -2, 2, 0))
        a = jnp.where(off > 2, FAR, jnp.where(off < -2, -FAR, 0))
        return plane(-off), k, a, off - a

    def c2_copy(n):
        i, k, a, b = group(n)
        return copy_to(cbuf.at[1, i], nbuf.at[k, b + 2], c2_s.at[n], c2_r.at[k, b + 2], y * Z + plane(-b), q)

    def c2_each(fn):
        def one(n):
            i, k, a, b = group(n)

            @pl.when((y == 0) | (i <= z))
            def _():
                fn(n, i, b)

        loop(0, Z, one)

    def c2_send(n, i, b):
        c1_wait(1, i)

        @pl.when((y == 0) & (i <= z))
        def _():
            c1_wait(0, i)
            cbuf[1, i] += cbuf[0, i]

        @pl.when(b != 0)
        def _():
            c2_copy(n).start()

    c2_each(c2_send)

    def c3_copy(k):
        return copy_to(psum.at[k], abuf.at[k - 1], c3_s.at[k - 1], c3_r.at[k - 1], y * Z + source(k)[0], q)

    def c3_sum(k):
        t, n = source(k)
        psum[k] = jnp.zeros((S, T), f32)

        @pl.when((y == 0) | (t <= z))
        def _():
            psum[k] = cbuf[1, t]

        def add(i):
            @pl.when((i != 2) & ((y == 0) | (t <= plane(i - 2))))
            def _():
                copy_to(nbuf.at[k, i], nbuf.at[k, i], c2_s.at[0], c2_r.at[k, i], p, q).wait_recv()
                psum[k] += nbuf[k, i]

        loop(0, n, add)


    sum_far_end(g_far, gs, gx)
    g_near = sum_near(gs, gx, gx_s, gx_r)
    for c in g_near:
        c.start()

    for h in range(2):
        @pl.when(q + h * NQ < p)
        def _():
            copy_to(vc.at[h], vc.at[h], v_s.at[0, 0], v_r.at[h], p, q).wait_recv()

    @pl.when(q <= p)
    def _():
        rpart[...] = dot(vc[0], low[0], 1, 1)

    @pl.when(q + NQ <= p)
    def _():
        rpart[...] += dot(vc[1], low[1], 1, 1)

    def row_copy(j):
        return copy_to(rows(rpart, j), rowbuf.at[q], row_s.at[j], row_r.at[q], p, j)

    @pl.when(q <= p)
    def _():
        loop(1, NQ, lambda d: row_copy(lax.rem(q + d, NQ)).start())
        rowbuf[q] = rpart[pl.ds(pl.multiple_of(q * S, S), S), :]

    for k in (1, 2):
        c3_sum(k)
        c3_copy(k).start()

    sum_near_end(g_far, g_near, gs, gx)
    all_send(gs, gram, ga_s, ga_r)
    c3_sum(0)

    wsl[...] = jnp.zeros((S, T), f32)

    def row_add(j):
        @pl.when(j != q)
        def _():
            copy_to(rowbuf.at[j], rowbuf.at[j], row_s.at[0], row_r.at[j], p, q).wait_recv()

        wsl[...] += rowbuf[j]

    loop(0, last_q + 1, row_add)
    ms[0] = dot(wsl[...], vp[...], 1, 1)
    m_far = sum_far(ms, mx, mx_s, mx_r)
    for c in m_far:
        c.start()

    for k in (1, 2):
        copy_to(abuf.at[k - 1], abuf.at[k - 1], c3_s.at[0], c3_r.at[k - 1], p, q).wait_recv()
    wsl[...] += (psum[0] + abuf[0]) + abuf[1]
    w_first = first(wsl, wrel, wf_s, wf_r)
    for c in w_first:
        c.start()
    fan(0, wsl, w_dst, w_s, w_r)

    def wrow_copy(j):
        return copy_to(wsl, rows(wp, q), wr_s.at[j], wr_r.at[q], p, j)

    loop(0, last_q + 1, lambda j: not_me(j, lambda i: wrow_copy(i).start()))
    wp[pl.ds(pl.multiple_of(q * S, S), S), :] = wsl[...]

    all_wait(gram, ga_s, ga_r)
    diag = jnp.where(ii == jj, 0.5 * gram[...], 0.0)
    power = jnp.where(ii < jj, -gram[...], 0.0) / jnp.sum(diag, axis=1, keepdims=True)
    stack[0:T] = jnp.where(ii == jj, 1.0, power)
    stack[T:] = dot(power, power)

    def double(_):
        both = dot(stack[...], stack[T:])
        stack[0:T] += both[0:T]
        stack[T:] = both[T:]

    loop(0, 4, double)

    sum_far_end(m_far, ms, mx)
    m_near = sum_near(ms, mx, mx_s, mx_r)
    for c in m_near:
        c.start()

    for k in (1, 2):
        relay(k, wrel, wf_s, wf_r, w_dst, w_s, w_r)

    loop(0, 2, double)
    coef[...] = (stack[0:T] + dot(stack[0:T], stack[T:])) / jnp.sum(diag, axis=0, keepdims=True)

    sum_near_end(m_far, m_near, ms, mx)
    all_send(ms, mtot, ma_s, ma_r)
    yp[...] = dot(coef[...], vp[...])
    lhs[T:] = -yp[...]
    for h in range(2):
        @pl.when(q + h * NQ <= p)
        def _():
            rhs[h, 0:T] = dot(coef[...], vc[h])

    @pl.when(q <= p)
    def _():
        def wr_wait(j):
            copy_to(rows(wp, j), rows(wp, j), wr_s.at[0], wr_r.at[j], p, q).wait_recv()

        loop(0, NQ, lambda j: not_me(j, wr_wait))
        lhs[0:T] = -wp[...]

    for h in range(2):
        c = q + h * NQ

        @pl.when(c < p)
        def _():
            copy_to(rhs.at[h, pl.ds(T, T)], rhs.at[h, pl.ds(T, T)], w_s.at[0, 0], w_r.at[h], p, q).wait_recv()

        @pl.when(c == p)
        def _():
            rhs[h, T:] = wp[...]

        @pl.when(c <= p)
        def _():
            tile = a_ref[:, h, :]
            sym = jnp.where(c < p, tile, 0.5 * (tile + tile.T))
            low[h] = sym + dot(lhs[...], rhs[h], 0, 0)

    all_wait(mtot, ma_s, ma_r)
    wp[...] = dot(mtot[...] + mtot[...].T, yp[...])
    for h in range(2):
        c = q + h * NQ

        @pl.when(c <= p)
        def _():
            o_ref[:, h, :] = low[h] + dot(wp[...], rhs[h, 0:T], 0, 0)

        @pl.when(c > p)
        def _():
            o_ref[:, h, :] = jnp.zeros((T, T), f32)

    for k, (v_src, w_src) in enumerate(((v_mine, wsl), (vrel.at[0], wrel.at[0]), (vrel.at[1], wrel.at[1]))):
        fan_done(k, v_src, v_dst, v_s, v_r)
        fan_done(k, w_src, w_dst, w_s, w_r)
    for h in range(2):
        @pl.when(q + h * NQ <= p)
        def _():
            c1_each(h, lambda c: c.wait_send())

    def c2_sent(n, i, b):
        @pl.when(b != 0)
        def _():
            c2_copy(n).wait_send()

    c2_each(c2_sent)
    for k in (1, 2):
        c3_copy(k).wait_send()

    @pl.when(q <= p)
    def _():
        loop(1, NQ, lambda d: row_copy(lax.rem(q + d, NQ)).wait_send())

    loop(0, last_q + 1, lambda j: not_me(j, lambda i: wrow_copy(i).wait_send()))
    loop(1, NQ, lambda d: all_copy(gs, gram, ga_s, ga_r, lax.rem(q + d, NQ)).wait_send())
    loop(1, NQ, lambda d: all_copy(ms, mtot, ma_s, ma_r, lax.rem(q + d, NQ)).wait_send())
    for c in v_first + w_first + g_far + g_near + m_far + m_near:
        c.wait_send()


def body(matrix, reflectors):
    vmem = lambda *shape: pltpu.VMEM(shape, f32)
    dma = lambda *shape: pltpu.SemaphoreType.DMA(shape)
    out = pl.pallas_call(
        kernel,
        out_shape=jax.ShapeDtypeStruct((T, 2, T), f32),
        in_specs=[pl.BlockSpec(memory_space=pltpu.HBM)] * 2,
        out_specs=pl.BlockSpec(memory_space=pltpu.VMEM),
        scratch_shapes=[
            vmem(T, 2, T), vmem(T, T),
            vmem(T, T), vmem(2, T, T), vmem(2, T, T), vmem(2, T, T),
            vmem(2, NQ, S, T), vmem(3, 6, S, T), vmem(3, S, T), vmem(2, S, T), vmem(NQ, S, T),
            vmem(T, T), vmem(S, T), vmem(T, T), vmem(2, S, T), vmem(2, S, T),
            vmem(3, S, T), vmem(11, S, T), vmem(T, T), vmem(3, S, T), vmem(11, S, T), vmem(T, T),
            vmem(2 * T, T), vmem(T, T), vmem(T, T), vmem(2 * T, T), vmem(2, 2 * T, T),
            dma(2), dma(3, 12), dma(2), dma(2), dma(2), dma(3, 12), dma(2), dma(2), dma(2),
            dma(2, NQ), dma(2, NQ), dma(Z), dma(3, 6), dma(2), dma(2), dma(NQ), dma(NQ), dma(NQ), dma(NQ),
            dma(11), dma(11), dma(NQ), dma(NQ), dma(11), dma(11), dma(NQ), dma(NQ),
        ],
        compiler_params=pltpu.CompilerParams(collective_id=0, has_side_effects=True, vmem_limit_bytes=60 * 2**20),
        cost_estimate=pl.CostEstimate(flops=34 * 2 * T**3, bytes_accessed=5 * T * T * 4, transcendentals=0),
    )(matrix.reshape(T, 2, T), reflectors.reshape(T, T))
    return out.reshape(matrix.shape)


def solution(mesh):
    placed = (P(None, "prow", None, "pcol"), P(None, "prow", None))
    return jax.shard_map(
        body, mesh=mesh, in_specs=placed, out_specs=P(None, "prow", None, "pcol"), check_vma=False
    )
```

```python
import jax
import jax.numpy as jnp
from jax import lax
from jax.experimental import pallas as pl
from jax.experimental.pallas import tpu as pltpu
from jax.sharding import PartitionSpec as P

MESH = pl.DeviceIdType.MESH
f32 = jnp.float32
NP, NQ, T, S = 32, 16, 256, 16
Z = 16
FAR = 5


def dot(a, b, ca=1, cb=0):
    return lax.dot_general(a, b, (((ca,), (cb,)), ((), ())), precision=lax.Precision.HIGHEST, preferred_element_type=f32)


def copy_to(src, dst, send_sem, recv_sem, p, q):
    return pltpu.make_async_remote_copy(
        src_ref=src, dst_ref=dst, send_sem=send_sem, recv_sem=recv_sem, device_id=(p, q), device_id_type=MESH
    )


def loop(lo, hi, fn):
    def step(i, carry):
        fn(i)
        return carry

    lax.fori_loop(lo, hi, step, 0)


def rows(ref, i, n=S):
    return ref.at[pl.ds(pl.multiple_of(i * n, n), n)]


def kernel(a_hbm, r_hbm, o_ref, a_ref, r_ref, vp, vc, low, pc, cbuf, nbuf, psum, abuf, rowbuf, rpart, wsl, wp, vrel, wrel,
           gs, gx, gram, ms, mx, mtot, stack, coef, yp, lhs, rhs,
           in_s, v_s, v_r, vf_s, vf_r, w_s, w_r, wf_s, wf_r, c1_s, c1_r, c2_s, c2_r, c3_s, c3_r, row_s, row_r, wr_s, wr_r,
           gx_s, gx_r, ga_s, ga_r, mx_s, mx_r, ma_s, ma_r):
    p = lax.axis_index("prow")
    q = lax.axis_index("pcol")
    y = p // Z
    z = lax.rem(p, Z)
    last_q = jnp.minimum(p, NQ - 1)
    get_r = pltpu.make_async_copy(r_hbm, r_ref, in_s.at[0])
    get_a = pltpu.make_async_copy(a_hbm, a_ref, in_s.at[1])
    get_r.start()
    get_a.start()

    def plane(d):
        return lax.rem(z + d + Z, Z)

    def not_me(j, fn):
        @pl.when(j != q)
        def _():
            fn(j)

    def source(k):
        return plane((0, -FAR, FAR)[k]), (5, 6, 5)[k]

    def targets(k, fn):
        t, n = source(k)

        def one(i):
            yy = lax.rem(i, 2)
            pp = yy * Z + plane(i // 2 - 2)
            fn(i, pp, t, pp > y * Z + t, (pp == p) & (t == q))

        loop(0, 2 * n, one)

    barrier = pltpu.get_barrier_semaphore()

    def greet(pp, qq):
        pl.semaphore_signal(barrier, inc=1, device_id=(pp, qq), device_id_type=MESH)

    for d in (FAR, -FAR):
        greet((1 - y) * Z + plane(d), q)
    loop(1, Z, lambda d: greet(y * Z + plane(d), q))
    off = lax.rem(z - q + 7 + Z, Z) - 7
    step = jnp.where(off < -2, -FAR, jnp.where(off > 2, FAR, 0))
    from_z = lax.rem(q + step + Z, Z)
    for h in range(2):
        @pl.when(q + h * NQ < p)
        def _():
            def hello(j):
                @pl.when((h != y) | (from_z != z) | (j != q))
                def _():
                    greet(h * Z + from_z, j)

            loop(0, NQ, hello)

    loop(1, NQ, lambda d: greet(p, lax.rem(q + d, NQ)))
    loop(0, NQ, lambda j: greet((1 - y) * Z + z, j))
    count = jnp.int32(17 + 31)
    for k in range(3):
        t, n = source(k)
        for i in range(2 * n):
            pp = (i % 2) * Z + plane(i // 2 - 2)
            count += ((pp > y * Z + t) & ((pp != p) | (t != q))).astype(jnp.int32)

    get_r.wait()
    raw = r_ref[...]
    ii = lax.broadcasted_iota(jnp.int32, (T, T), 0)
    jj = lax.broadcasted_iota(jnp.int32, (T, T), 1)
    unit = jnp.where(ii > jj, raw, jnp.where(ii == jj, 1.0, 0.0))
    vp[...] = jnp.where(p == 0, 0.0, jnp.where(p == 1, unit, raw)).T
    gs[0] = dot(vp[pl.ds(pl.multiple_of(q * S, S), S), :], vp[...], 1, 1)
    get_a.wait()
    for h in range(2):
        c = q + h * NQ

        @pl.when(c <= p)
        def _():
            tile = a_ref[:, h, :] * jnp.where(c < p, 1.0, 0.5)
            low[h] = tile
            pc[h] = dot(vp[...], tile)

        @pl.when(c == p)
        def _():
            vc[h] = vp[...]

    pl.semaphore_wait(barrier, count)

    def first(src, rel, f_s, f_r):
        return [
            copy_to(src, rel.at[0], f_s.at[0], f_r.at[0], y * Z + plane(FAR), q),
            copy_to(src, rel.at[1], f_s.at[1], f_r.at[1], y * Z + plane(-FAR), q),
        ]

    def fan(k, src, dst, s_s, s_r):
        def send(i, pp, t, live, me):
            @pl.when(live & jnp.logical_not(me))
            def _():
                copy_to(src, dst, s_s.at[k, i], s_r.at[y], pp, t).start()

            @pl.when(live & me)
            def _():
                pltpu.make_async_copy(src, dst, s_r.at[y]).start()

        targets(k, send)

    def fan_done(k, src, dst, s_s, s_r):
        def done(i, pp, t, live, me):
            @pl.when(live & jnp.logical_not(me))
            def _():
                copy_to(src, dst, s_s.at[k, i], s_r.at[y], pp, t).wait_send()

        targets(k, done)

    v_mine = rows(vp, q)
    v_dst = rows(vc.at[y], q)
    w_dst = rhs.at[y, pl.ds(pl.multiple_of(T + q * S, S), S)]
    v_first = first(v_mine, vrel, vf_s, vf_r)
    for c in v_first:
        c.start()
    fan(0, v_mine, v_dst, v_s, v_r)

    def c1_copy(h, j):
        return copy_to(rows(pc.at[h], j), cbuf.at[y, q], c1_s.at[h, j], c1_r.at[y, q], h * Z + z, j)

    def c1_each(h, fn):
        def one(d):
            j = lax.rem(q + d, NQ)

            @pl.when((h != y) | (j != q))
            def _():
                fn(c1_copy(h, j))

        loop(0, NQ, one)

    for h in range(2):
        @pl.when(q + h * NQ <= p)
        def _():
            c1_each(h, lambda c: c.start())

            @pl.when(h == y)
            def _():
                cbuf[y, q] = pc[h, pl.ds(pl.multiple_of(q * S, S), S), :]


    def sum_pair(buf, got, s, r):
        return copy_to(buf.at[0], got.at[4], s.at[4], r.at[4], (1 - y) * Z + z, q)

    def sum_far(buf, stage, got, s, r, pairs):
        return [
            copy_to(buf.at[stage], got.at[k], s.at[k], r.at[k], (1 - y if k > 1 else y) * Z + plane((FAR, -FAR)[k % 2]), q)
            for k in range(4 if pairs else 2)
        ]

    def sum_near(buf, got, s, r):
        return [
            copy_to(buf.at[3 if k == 0 else 2], got.at[5 + k], s.at[5 + k], r.at[5 + k], y * Z + plane(d), q)
            for k, d in enumerate((-3, -2, 2, -1, 1))
        ]

    def sum_far_end(copies, stage, buf, got):
        for c in copies:
            c.wait_recv()
        above = [got[k] for k in range(len(copies)) if k % 2 == 1]
        below = [got[k] for k in range(len(copies)) if k % 2 == 0]
        buf[2] = (buf[stage] + sum(above)) + sum(below)
        buf[3] = sum(above)

    def sum_near_end(copies, buf, got):
        total = buf[2]
        for k, c in enumerate(copies):
            c.wait_recv()
            total += got[5 + k]
        buf[4] = total

    def all_copy(buf, dst, s, r, j):
        return copy_to(buf.at[4], rows(dst, q), s.at[j], r.at[q], p, j)

    def all_send(buf, dst, s, r):
        loop(1, NQ, lambda d: all_copy(buf, dst, s, r, lax.rem(q + d, NQ)).start())
        dst[pl.ds(pl.multiple_of(q * S, S), S), :] = buf[4]

    def all_wait(dst, s, r):
        def one(j):
            copy_to(rows(dst, j), rows(dst, j), s.at[0], r.at[j], p, q).wait_recv()

        loop(0, NQ, lambda j: not_me(j, one))

    g_pair = sum_pair(gs, gx, gx_s, gx_r)
    g_pair.start()
    g_pair.wait_recv()
    gs[1] = gs[0] + gx[4]
    g_far = sum_far(gs, 1, gx, gx_s, gx_r, False)
    for c in g_far:
        c.start()

    def relay(k, rel, f_s, f_r, dst, s_s, s_r):
        copy_to(rel.at[k - 1], rel.at[k - 1], f_s.at[k - 1], f_r.at[k - 1], p, q).wait_recv()
        fan(k, rel.at[k - 1], dst, s_s, s_r)

    for k in (1, 2):
        relay(k, vrel, vf_s, vf_r, v_dst, v_s, v_r)

    def c1_wait(yy, i):
        @pl.when((yy != y) | (i != q))
        def _():
            copy_to(cbuf.at[yy, i], cbuf.at[yy, i], c1_s.at[0, 0], c1_r.at[yy, i], p, q).wait_recv()

    def group(n):
        off = jnp.where(n < 6, n + 3, jnp.where(n < 11, 3 - n, n - 13))
        k = jnp.where(off > 2, 1, jnp.where(off < -2, 2, 0))
        a = jnp.where(off > 2, FAR, jnp.where(off < -2, -FAR, 0))
        return plane(-off), k, a, off - a

    def c2_copy(n):
        i, k, a, b = group(n)
        return copy_to(cbuf.at[1, i], nbuf.at[k, b + 2], c2_s.at[n], c2_r.at[k, b + 2], y * Z + plane(-b), q)

    def c2_each(fn):
        def one(n):
            i, k, a, b = group(n)

            @pl.when((y == 0) | (i <= z))
            def _():
                fn(n, i, b)

        loop(0, Z, one)

    def c2_send(n, i, b):
        c1_wait(1, i)

        @pl.when((y == 0) & (i <= z))
        def _():
            c1_wait(0, i)
            cbuf[1, i] += cbuf[0, i]

        @pl.when(b != 0)
        def _():
            c2_copy(n).start()

    c2_each(c2_send)

    def c3_copy(k):
        return copy_to(psum.at[k], abuf.at[k - 1], c3_s.at[k - 1], c3_r.at[k - 1], y * Z + source(k)[0], q)

    def c3_sum(k):
        t, n = source(k)
        psum[k] = jnp.zeros((S, T), f32)

        @pl.when((y == 0) | (t <= z))
        def _():
            psum[k] = cbuf[1, t]

        def add(i):
            @pl.when((i != 2) & ((y == 0) | (t <= plane(i - 2))))
            def _():
                copy_to(nbuf.at[k, i], nbuf.at[k, i], c2_s.at[0], c2_r.at[k, i], p, q).wait_recv()
                psum[k] += nbuf[k, i]

        loop(0, n, add)


    sum_far_end(g_far, 1, gs, gx)
    g_near = sum_near(gs, gx, gx_s, gx_r)
    for c in g_near:
        c.start()

    for h in range(2):
        @pl.when(q + h * NQ < p)
        def _():
            copy_to(vc.at[h], vc.at[h], v_s.at[0, 0], v_r.at[h], p, q).wait_recv()

    @pl.when(q <= p)
    def _():
        rpart[...] = dot(vc[0], low[0], 1, 1)

    @pl.when(q + NQ <= p)
    def _():
        rpart[...] += dot(vc[1], low[1], 1, 1)

    def row_copy(j):
        return copy_to(rows(rpart, j), rowbuf.at[q], row_s.at[j], row_r.at[q], p, j)

    @pl.when(q <= p)
    def _():
        loop(1, NQ, lambda d: row_copy(lax.rem(q + d, NQ)).start())
        rowbuf[q] = rpart[pl.ds(pl.multiple_of(q * S, S), S), :]

    for k in (1, 2):
        c3_sum(k)
        c3_copy(k).start()

    sum_near_end(g_near, gs, gx)
    all_send(gs, gram, ga_s, ga_r)
    c3_sum(0)

    wsl[...] = jnp.zeros((S, T), f32)

    def row_add(j):
        @pl.when(j != q)
        def _():
            copy_to(rowbuf.at[j], rowbuf.at[j], row_s.at[0], row_r.at[j], p, q).wait_recv()

        wsl[...] += rowbuf[j]

    loop(0, last_q + 1, row_add)
    ms[0] = dot(wsl[...], vp[...], 1, 1)
    m_far = sum_far(ms, 0, mx, mx_s, mx_r, True)
    m_pair = sum_pair(ms, mx, mx_s, mx_r)
    for c in m_far + [m_pair]:
        c.start()

    for k in (1, 2):
        copy_to(abuf.at[k - 1], abuf.at[k - 1], c3_s.at[0], c3_r.at[k - 1], p, q).wait_recv()
    wsl[...] += (psum[0] + abuf[0]) + abuf[1]
    w_first = first(wsl, wrel, wf_s, wf_r)
    for c in w_first:
        c.start()
    fan(0, wsl, w_dst, w_s, w_r)

    def wrow_copy(j):
        return copy_to(wsl, rows(wp, q), wr_s.at[j], wr_r.at[q], p, j)

    loop(0, last_q + 1, lambda j: not_me(j, lambda i: wrow_copy(i).start()))
    wp[pl.ds(pl.multiple_of(q * S, S), S), :] = wsl[...]

    all_wait(gram, ga_s, ga_r)
    diag = jnp.where(ii == jj, 0.5 * gram[...], 0.0)
    power = jnp.where(ii < jj, -gram[...], 0.0) / jnp.sum(diag, axis=1, keepdims=True)
    stack[0:T] = jnp.where(ii == jj, 1.0, power)
    stack[T:] = dot(power, power)

    def double(_):
        both = dot(stack[...], stack[T:])
        stack[0:T] += both[0:T]
        stack[T:] = both[T:]

    loop(0, 4, double)

    m_pair.wait_recv()
    ms[1] = ms[0] + mx[4]
    sum_far_end(m_far, 1, ms, mx)
    m_near = sum_near(ms, mx, mx_s, mx_r)
    for c in m_near:
        c.start()

    for k in (1, 2):
        relay(k, wrel, wf_s, wf_r, w_dst, w_s, w_r)

    loop(0, 2, double)
    coef[...] = (stack[0:T] + dot(stack[0:T], stack[T:])) / jnp.sum(diag, axis=0, keepdims=True)

    sum_near_end(m_near, ms, mx)
    all_send(ms, mtot, ma_s, ma_r)
    yp[...] = dot(coef[...], vp[...])
    lhs[T:] = -yp[...]
    for h in range(2):
        @pl.when(q + h * NQ <= p)
        def _():
            rhs[h, 0:T] = dot(coef[...], vc[h])

    @pl.when(q <= p)
    def _():
        def wr_wait(j):
            copy_to(rows(wp, j), rows(wp, j), wr_s.at[0], wr_r.at[j], p, q).wait_recv()

        loop(0, NQ, lambda j: not_me(j, wr_wait))
        lhs[0:T] = -wp[...]

    for h in range(2):
        c = q + h * NQ

        @pl.when(c < p)
        def _():
            copy_to(rhs.at[h, pl.ds(T, T)], rhs.at[h, pl.ds(T, T)], w_s.at[0, 0], w_r.at[h], p, q).wait_recv()

        @pl.when(c == p)
        def _():
            rhs[h, T:] = wp[...]

        @pl.when(c <= p)
        def _():
            tile = a_ref[:, h, :]
            sym = jnp.where(c < p, tile, 0.5 * (tile + tile.T))
            low[h] = sym + dot(lhs[...], rhs[h], 0, 0)

    all_wait(mtot, ma_s, ma_r)
    wp[...] = dot(mtot[...] + mtot[...].T, yp[...])
    for h in range(2):
        c = q + h * NQ

        @pl.when(c <= p)
        def _():
            o_ref[:, h, :] = low[h] + dot(wp[...], rhs[h, 0:T], 0, 0)

        @pl.when(c > p)
        def _():
            o_ref[:, h, :] = jnp.zeros((T, T), f32)

    for k, (v_src, w_src) in enumerate(((v_mine, wsl), (vrel.at[0], wrel.at[0]), (vrel.at[1], wrel.at[1]))):
        fan_done(k, v_src, v_dst, v_s, v_r)
        fan_done(k, w_src, w_dst, w_s, w_r)
    for h in range(2):
        @pl.when(q + h * NQ <= p)
        def _():
            c1_each(h, lambda c: c.wait_send())

    def c2_sent(n, i, b):
        @pl.when(b != 0)
        def _():
            c2_copy(n).wait_send()

    c2_each(c2_sent)
    for k in (1, 2):
        c3_copy(k).wait_send()

    @pl.when(q <= p)
    def _():
        loop(1, NQ, lambda d: row_copy(lax.rem(q + d, NQ)).wait_send())

    loop(0, last_q + 1, lambda j: not_me(j, lambda i: wrow_copy(i).wait_send()))
    loop(1, NQ, lambda d: all_copy(gs, gram, ga_s, ga_r, lax.rem(q + d, NQ)).wait_send())
    loop(1, NQ, lambda d: all_copy(ms, mtot, ma_s, ma_r, lax.rem(q + d, NQ)).wait_send())
    for c in v_first + w_first + g_far + g_near + m_far + m_near + [g_pair, m_pair]:
        c.wait_send()


def body(matrix, reflectors):
    vmem = lambda *shape: pltpu.VMEM(shape, f32)
    dma = lambda *shape: pltpu.SemaphoreType.DMA(shape)
    out = pl.pallas_call(
        kernel,
        out_shape=jax.ShapeDtypeStruct((T, 2, T), f32),
        in_specs=[pl.BlockSpec(memory_space=pltpu.HBM)] * 2,
        out_specs=pl.BlockSpec(memory_space=pltpu.VMEM),
        scratch_shapes=[
            vmem(T, 2, T), vmem(T, T),
            vmem(T, T), vmem(2, T, T), vmem(2, T, T), vmem(2, T, T),
            vmem(2, NQ, S, T), vmem(3, 6, S, T), vmem(3, S, T), vmem(2, S, T), vmem(NQ, S, T),
            vmem(T, T), vmem(S, T), vmem(T, T), vmem(2, S, T), vmem(2, S, T),
            vmem(5, S, T), vmem(10, S, T), vmem(T, T), vmem(5, S, T), vmem(10, S, T), vmem(T, T),
            vmem(2 * T, T), vmem(T, T), vmem(T, T), vmem(2 * T, T), vmem(2, 2 * T, T),
            dma(2), dma(3, 12), dma(2), dma(2), dma(2), dma(3, 12), dma(2), dma(2), dma(2),
            dma(2, NQ), dma(2, NQ), dma(Z), dma(3, 6), dma(2), dma(2), dma(NQ), dma(NQ), dma(NQ), dma(NQ),
            dma(10), dma(10), dma(NQ), dma(NQ), dma(10), dma(10), dma(NQ), dma(NQ),
        ],
        compiler_params=pltpu.CompilerParams(collective_id=0, has_side_effects=True, vmem_limit_bytes=53 * 2**20),
        cost_estimate=pl.CostEstimate(flops=34 * 2 * T**3, bytes_accessed=5 * T * T * 4, transcendentals=0),
    )(matrix.reshape(T, 2, T), reflectors.reshape(T, T))
    return out.reshape(matrix.shape)


def solution(mesh):
    placed = (P(None, "prow", None, "pcol"), P(None, "prow", None))
    return jax.shard_map(
        body, mesh=mesh, in_specs=placed, out_specs=P(None, "prow", None, "pcol"), check_vma=False
    )
```

```python
import jax
import jax.numpy as jnp
from jax import lax
from jax.experimental import pallas as pl
from jax.experimental.pallas import tpu as pltpu
from jax.sharding import PartitionSpec as P

MESH = pl.DeviceIdType.MESH
f32 = jnp.float32
NP, NQ, T, S = 32, 16, 256, 16
H = S // 2
Z = 16
FAR = 5


def dot(a, b, ca=1, cb=0):
    return lax.dot_general(a, b, (((ca,), (cb,)), ((), ())), precision=lax.Precision.HIGHEST, preferred_element_type=f32)


def copy_to(src, dst, send_sem, recv_sem, p, q):
    return pltpu.make_async_remote_copy(
        src_ref=src, dst_ref=dst, send_sem=send_sem, recv_sem=recv_sem, device_id=(p, q), device_id_type=MESH
    )


def loop(lo, hi, fn):
    def step(i, carry):
        fn(i)
        return carry

    lax.fori_loop(lo, hi, step, 0)


def rows(ref, i, n=S):
    return ref.at[pl.ds(pl.multiple_of(i * n, n), n)]


def kernel(a_hbm, r_hbm, o_ref, a_ref, r_ref, vp, vc, low, pc, cbuf, nbuf, psum, abuf, rowbuf, rpart, wsl, wp, vrel, wrel,
           gterm, gs, gx, gram, mterm, ms, mx, mtot, stack, coef, yp, lhs, rhs,
           in_s, v_s, v_r, vf_s, vf_r, w_s, w_r, wf_s, wf_r, c1_s, c1_r, c2_s, c2_r, c3_s, c3_r, row_s, row_r, wr_s, wr_r,
           gx_s, gx_r, ga_s, ga_r, mx_s, mx_r, ma_s, ma_r):
    p = lax.axis_index("prow")
    q = lax.axis_index("pcol")
    y = p // Z
    z = lax.rem(p, Z)
    mate = q + 1 - 2 * lax.rem(q, 2)
    last_q = jnp.minimum(p, NQ - 1)
    get_r = pltpu.make_async_copy(r_hbm, r_ref, in_s.at[0])
    get_a = pltpu.make_async_copy(a_hbm, a_ref, in_s.at[1])
    get_r.start()
    get_a.start()

    def plane(d):
        return lax.rem(z + d + Z, Z)

    def not_me(j, fn):
        @pl.when(j != q)
        def _():
            fn(j)

    def source(k):
        return plane((0, -FAR, FAR)[k]), (5, 6, 5)[k]

    def targets(k, fn):
        t, n = source(k)

        def one(i):
            yy = lax.rem(i, 2)
            pp = yy * Z + plane(i // 2 - 2)
            fn(i, pp, t, pp > y * Z + t, (pp == p) & (t == q))

        loop(0, 2 * n, one)

    barrier = pltpu.get_barrier_semaphore()

    def greet(pp, qq):
        pl.semaphore_signal(barrier, inc=1, device_id=(pp, qq), device_id_type=MESH)

    for d in (FAR, -FAR):
        greet((1 - y) * Z + plane(d), q)
    for d in (FAR, -FAR, 3, 2, -2, 1, -1):
        greet(y * Z + plane(d), q)
    off = lax.rem(z - q + 7 + Z, Z) - 7
    step = jnp.where(off < -2, -FAR, jnp.where(off > 2, FAR, 0))
    from_z = lax.rem(q + step + Z, Z)
    for h in range(2):
        @pl.when(q + h * NQ < p)
        def _():
            def hello(j):
                @pl.when((h != y) | (from_z != z) | (j != q))
                def _():
                    greet(h * Z + from_z, j)

            loop(0, NQ, hello)

    loop(1, NQ, lambda d: greet(p, lax.rem(q + d, NQ)))
    loop(0, NQ, lambda j: greet((1 - y) * Z + z, j))
    count = jnp.int32(9 + 31)
    for k in range(3):
        t, n = source(k)
        for i in range(2 * n):
            pp = (i % 2) * Z + plane(i // 2 - 2)
            count += ((pp > y * Z + t) & ((pp != p) | (t != q))).astype(jnp.int32)

    get_r.wait()
    raw = r_ref[...]
    ii = lax.broadcasted_iota(jnp.int32, (T, T), 0)
    jj = lax.broadcasted_iota(jnp.int32, (T, T), 1)
    unit = jnp.where(ii > jj, raw, jnp.where(ii == jj, 1.0, 0.0))
    vp[...] = jnp.where(p == 0, 0.0, jnp.where(p == 1, unit, raw)).T
    gterm[...] = dot(vp[pl.ds(pl.multiple_of(q * S, S), S), :], vp[...], 1, 1)
    get_a.wait()
    for h in range(2):
        c = q + h * NQ

        @pl.when(c <= p)
        def _():
            tile = a_ref[:, h, :] * jnp.where(c < p, 1.0, 0.5)
            low[h] = tile
            pc[h] = dot(vp[...], tile)

        @pl.when(c == p)
        def _():
            vc[h] = vp[...]

    pl.semaphore_wait(barrier, count)

    def first(src, rel, f_s, f_r):
        return [
            copy_to(src, rel.at[0], f_s.at[0], f_r.at[0], y * Z + plane(FAR), q),
            copy_to(src, rel.at[1], f_s.at[1], f_r.at[1], y * Z + plane(-FAR), q),
        ]

    def fan(k, src, dst, s_s, s_r):
        def send(i, pp, t, live, me):
            @pl.when(live & jnp.logical_not(me))
            def _():
                copy_to(src, dst, s_s.at[k, i], s_r.at[y], pp, t).start()

            @pl.when(live & me)
            def _():
                pltpu.make_async_copy(src, dst, s_r.at[y]).start()

        targets(k, send)

    def fan_done(k, src, dst, s_s, s_r):
        def done(i, pp, t, live, me):
            @pl.when(live & jnp.logical_not(me))
            def _():
                copy_to(src, dst, s_s.at[k, i], s_r.at[y], pp, t).wait_send()

        targets(k, done)

    v_mine = rows(vp, q)
    v_dst = rows(vc.at[y], q)
    w_dst = rhs.at[y, pl.ds(pl.multiple_of(T + q * S, S), S)]
    v_first = first(v_mine, vrel, vf_s, vf_r)
    for c in v_first:
        c.start()
    fan(0, v_mine, v_dst, v_s, v_r)

    def c1_copy(h, j):
        return copy_to(rows(pc.at[h], j), cbuf.at[y, q], c1_s.at[h, j], c1_r.at[y, q], h * Z + z, j)

    def c1_each(h, fn):
        def one(d):
            j = lax.rem(q + d, NQ)

            @pl.when((h != y) | (j != q))
            def _():
                fn(c1_copy(h, j))

        loop(0, NQ, one)

    for h in range(2):
        @pl.when(q + h * NQ <= p)
        def _():
            c1_each(h, lambda c: c.start())

            @pl.when(h == y)
            def _():
                cbuf[y, q] = pc[h, pl.ds(pl.multiple_of(q * S, S), S), :]


    def sum_far(term, got, s, r):
        out = []
        for k, (d, yy) in enumerate(((FAR, y), (-FAR, y), (FAR, 1 - y), (-FAR, 1 - y), (0, 1 - y))):
            out.append(copy_to(rows(term, yy, H), got.at[k], s.at[k], r.at[k], yy * Z + plane(d), q))
        return out

    def sum_far_end(copies, term, buf, got):
        for c in copies:
            c.wait_recv()
        above = got[1] + got[3]
        buf[0] = (term[pl.ds(pl.multiple_of(y * H, H), H), :] + above) + (got[0] + got[2] + got[4])
        buf[1] = above

    def sum_near(buf, got, s, r):
        return [
            copy_to(buf.at[1 if k == 0 else 0], got.at[5 + k], s.at[5 + k], r.at[5 + k], y * Z + plane(d), q)
            for k, d in enumerate((-3, -2, 2, -1, 1))
        ]

    def sum_near_end(copies, buf, got):
        total = buf[0]
        for k, c in enumerate(copies):
            c.wait_recv()
            total += got[5 + k]
        buf[2] = total

    def all_send(buf, dst, s, r):
        def one(d):
            i = lax.rem(y * NQ + q + d, 2 * NQ)
            copy_to(buf.at[2], rows(dst, 2 * q + y, H), s.at[0], r.at[0], i // NQ * Z + z, lax.rem(i, NQ)).start()

        loop(1, 2 * NQ, one)
        dst[pl.ds(pl.multiple_of((2 * q + y) * H, H), H), :] = buf[2]

    def all_rows(dst, s, r):
        return copy_to(dst.at[pl.ds(0, T - H)], dst.at[pl.ds(0, T - H)], s.at[0], r.at[0], p, mate)

    g_far = sum_far(gterm, gx, gx_s, gx_r)
    for c in g_far:
        c.start()

    def relay(k, rel, f_s, f_r, dst, s_s, s_r):
        copy_to(rel.at[k - 1], rel.at[k - 1], f_s.at[k - 1], f_r.at[k - 1], p, q).wait_recv()
        fan(k, rel.at[k - 1], dst, s_s, s_r)

    for k in (1, 2):
        relay(k, vrel, vf_s, vf_r, v_dst, v_s, v_r)

    def c1_wait(yy, i):
        @pl.when((yy != y) | (i != q))
        def _():
            copy_to(cbuf.at[yy, i], cbuf.at[yy, i], c1_s.at[0, 0], c1_r.at[yy, i], p, q).wait_recv()

    def group(n):
        off = jnp.where(n < 6, n + 3, jnp.where(n < 11, 3 - n, n - 13))
        k = jnp.where(off > 2, 1, jnp.where(off < -2, 2, 0))
        a = jnp.where(off > 2, FAR, jnp.where(off < -2, -FAR, 0))
        return plane(-off), k, a, off - a

    def c2_copy(n):
        i, k, a, b = group(n)
        return copy_to(cbuf.at[1, i], nbuf.at[k, b + 2], c2_s.at[n], c2_r.at[k, b + 2], y * Z + plane(-b), q)

    def c2_each(fn):
        def one(n):
            i, k, a, b = group(n)

            @pl.when((y == 0) | (i <= z))
            def _():
                fn(n, i, b)

        loop(0, Z, one)

    def c2_send(n, i, b):
        c1_wait(1, i)

        @pl.when((y == 0) & (i <= z))
        def _():
            c1_wait(0, i)
            cbuf[1, i] += cbuf[0, i]

        @pl.when(b != 0)
        def _():
            c2_copy(n).start()

    c2_each(c2_send)

    def c3_copy(k):
        return copy_to(psum.at[k], abuf.at[k - 1], c3_s.at[k - 1], c3_r.at[k - 1], y * Z + source(k)[0], q)

    def c3_sum(k):
        t, n = source(k)
        psum[k] = jnp.zeros((S, T), f32)

        @pl.when((y == 0) | (t <= z))
        def _():
            psum[k] = cbuf[1, t]

        def add(i):
            @pl.when((i != 2) & ((y == 0) | (t <= plane(i - 2))))
            def _():
                copy_to(nbuf.at[k, i], nbuf.at[k, i], c2_s.at[0], c2_r.at[k, i], p, q).wait_recv()
                psum[k] += nbuf[k, i]

        loop(0, n, add)


    sum_far_end(g_far, gterm, gs, gx)
    g_near = sum_near(gs, gx, gx_s, gx_r)
    for c in g_near:
        c.start()

    for h in range(2):
        @pl.when(q + h * NQ < p)
        def _():
            copy_to(vc.at[h], vc.at[h], v_s.at[0, 0], v_r.at[h], p, q).wait_recv()

    @pl.when(q <= p)
    def _():
        rpart[...] = dot(vc[0], low[0], 1, 1)

    @pl.when(q + NQ <= p)
    def _():
        rpart[...] += dot(vc[1], low[1], 1, 1)

    def row_copy(j):
        return copy_to(rows(rpart, j), rowbuf.at[q], row_s.at[j], row_r.at[q], p, j)

    @pl.when(q <= p)
    def _():
        loop(1, NQ, lambda d: row_copy(lax.rem(q + d, NQ)).start())
        rowbuf[q] = rpart[pl.ds(pl.multiple_of(q * S, S), S), :]

    for k in (1, 2):
        c3_sum(k)
        c3_copy(k).start()

    sum_near_end(g_near, gs, gx)
    all_send(gs, gram, ga_s, ga_r)
    c3_sum(0)

    wsl[...] = jnp.zeros((S, T), f32)

    def row_add(j):
        @pl.when(j != q)
        def _():
            copy_to(rowbuf.at[j], rowbuf.at[j], row_s.at[0], row_r.at[j], p, q).wait_recv()

        wsl[...] += rowbuf[j]

    loop(0, last_q + 1, row_add)
    mterm[...] = dot(wsl[...], vp[...], 1, 1)
    m_far = sum_far(mterm, mx, mx_s, mx_r)
    for c in m_far:
        c.start()

    for k in (1, 2):
        copy_to(abuf.at[k - 1], abuf.at[k - 1], c3_s.at[0], c3_r.at[k - 1], p, q).wait_recv()
    wsl[...] += (psum[0] + abuf[0]) + abuf[1]
    w_first = first(wsl, wrel, wf_s, wf_r)
    for c in w_first:
        c.start()
    fan(0, wsl, w_dst, w_s, w_r)

    def wrow_copy(j):
        return copy_to(wsl, rows(wp, q), wr_s.at[j], wr_r.at[0], p, j)

    loop(0, last_q + 1, lambda j: not_me(j, lambda i: wrow_copy(i).start()))
    wp[pl.ds(pl.multiple_of(q * S, S), S), :] = wsl[...]

    for k, src in enumerate((v_mine, vrel.at[0], vrel.at[1])):
        fan_done(k, src, v_dst, v_s, v_r)
    for h in range(2):
        @pl.when(q + h * NQ <= p)
        def _():
            c1_each(h, lambda c: c.wait_send())

    def c2_sent(n, i, b):
        @pl.when(b != 0)
        def _():
            c2_copy(n).wait_send()

    c2_each(c2_sent)
    for k in (1, 2):
        c3_copy(k).wait_send()

    @pl.when(q <= p)
    def _():
        loop(1, NQ, lambda d: row_copy(lax.rem(q + d, NQ)).wait_send())

    for c in v_first + g_far + g_near:
        c.wait_send()

    all_rows(gram, ga_s, ga_r).wait_recv()
    diag = jnp.where(ii == jj, 0.5 * gram[...], 0.0)
    power = jnp.where(ii < jj, -gram[...], 0.0) / jnp.sum(diag, axis=1, keepdims=True)
    stack[0:T] = jnp.where(ii == jj, 1.0, power)
    stack[T:] = dot(power, power)

    def double(_):
        both = dot(stack[...], stack[T:])
        stack[0:T] += both[0:T]
        stack[T:] = both[T:]

    loop(0, 4, double)

    sum_far_end(m_far, mterm, ms, mx)
    m_near = sum_near(ms, mx, mx_s, mx_r)
    for c in m_near:
        c.start()

    for k in (1, 2):
        relay(k, wrel, wf_s, wf_r, w_dst, w_s, w_r)

    loop(0, 2, double)
    coef[...] = (stack[0:T] + dot(stack[0:T], stack[T:])) / jnp.sum(diag, axis=0, keepdims=True)

    sum_near_end(m_near, ms, mx)
    all_send(ms, mtot, ma_s, ma_r)
    yp[...] = dot(coef[...], vp[...])
    lhs[T:] = -yp[...]
    for h in range(2):
        @pl.when(q + h * NQ <= p)
        def _():
            rhs[h, 0:T] = dot(coef[...], vc[h])

    @pl.when(q <= p)
    def _():
        others = wp.at[pl.ds(0, T - S)]
        copy_to(others, others, wr_s.at[0], wr_r.at[0], p, mate).wait_recv()
        lhs[0:T] = -wp[...]

    for h in range(2):
        c = q + h * NQ

        @pl.when(c < p)
        def _():
            copy_to(rhs.at[h, pl.ds(T, T)], rhs.at[h, pl.ds(T, T)], w_s.at[0, 0], w_r.at[h], p, q).wait_recv()

        @pl.when(c == p)
        def _():
            rhs[h, T:] = wp[...]

        @pl.when(c <= p)
        def _():
            tile = a_ref[:, h, :]
            sym = jnp.where(c < p, tile, 0.5 * (tile + tile.T))
            low[h] = sym + dot(lhs[...], rhs[h], 0, 0)

    for k, src in enumerate((wsl, wrel.at[0], wrel.at[1])):
        fan_done(k, src, w_dst, w_s, w_r)
    loop(0, last_q + 1, lambda j: not_me(j, lambda i: wrow_copy(i).wait_send()))
    all_rows(gram, ga_s, ga_r).wait_send()
    for c in w_first + m_far + m_near:
        c.wait_send()

    all_rows(mtot, ma_s, ma_r).wait_recv()
    wp[...] = dot(mtot[...] + mtot[...].T, yp[...])
    for h in range(2):
        c = q + h * NQ

        @pl.when(c <= p)
        def _():
            o_ref[:, h, :] = low[h] + dot(wp[...], rhs[h, 0:T], 0, 0)

        @pl.when(c > p)
        def _():
            o_ref[:, h, :] = jnp.zeros((T, T), f32)

    all_rows(mtot, ma_s, ma_r).wait_send()


def body(matrix, reflectors):
    vmem = lambda *shape: pltpu.VMEM(shape, f32)
    dma = lambda *shape: pltpu.SemaphoreType.DMA(shape)
    out = pl.pallas_call(
        kernel,
        out_shape=jax.ShapeDtypeStruct((T, 2, T), f32),
        in_specs=[pl.BlockSpec(memory_space=pltpu.HBM)] * 2,
        out_specs=pl.BlockSpec(memory_space=pltpu.VMEM),
        scratch_shapes=[
            vmem(T, 2, T), vmem(T, T),
            vmem(T, T), vmem(2, T, T), vmem(2, T, T), vmem(2, T, T),
            vmem(2, NQ, S, T), vmem(3, 6, S, T), vmem(3, S, T), vmem(2, S, T), vmem(NQ, S, T),
            vmem(T, T), vmem(S, T), vmem(T, T), vmem(2, S, T), vmem(2, S, T),
            vmem(S, T), vmem(3, H, T), vmem(10, H, T), vmem(T, T),
            vmem(S, T), vmem(3, H, T), vmem(10, H, T), vmem(T, T),
            vmem(2 * T, T), vmem(T, T), vmem(T, T), vmem(2 * T, T), vmem(2, 2 * T, T),
            dma(2), dma(3, 12), dma(2), dma(2), dma(2), dma(3, 12), dma(2), dma(2), dma(2),
            dma(2, NQ), dma(2, NQ), dma(Z), dma(3, 6), dma(2), dma(2), dma(NQ), dma(NQ), dma(NQ), dma(1),
            dma(10), dma(10), dma(1), dma(1), dma(10), dma(10), dma(1), dma(1),
        ],
        compiler_params=pltpu.CompilerParams(collective_id=0, has_side_effects=True, vmem_limit_bytes=53 * 2**20),
        cost_estimate=pl.CostEstimate(flops=34 * 2 * T**3, bytes_accessed=5 * T * T * 4, transcendentals=0),
    )(matrix.reshape(T, 2, T), reflectors.reshape(T, T))
    return out.reshape(matrix.shape)


def solution(mesh):
    placed = (P(None, "prow", None, "pcol"), P(None, "prow", None))
    return jax.shard_map(
        body, mesh=mesh, in_specs=placed, out_specs=P(None, "prow", None, "pcol"), check_vma=False
    )
```

```python
import jax
import jax.numpy as jnp
from jax import lax
from jax.experimental import pallas as pl
from jax.experimental.pallas import tpu as pltpu
from jax.sharding import PartitionSpec as P

MESH = pl.DeviceIdType.MESH
f32 = jnp.float32
NP, NQ, T, S = 32, 16, 256, 16
H = S // 2
Z = 16
FAR = 5


def dot(a, b, ca=1, cb=0):
    return lax.dot_general(a, b, (((ca,), (cb,)), ((), ())), precision=lax.Precision.HIGHEST, preferred_element_type=f32)


def copy_to(src, dst, send_sem, recv_sem, p, q):
    return pltpu.make_async_remote_copy(
        src_ref=src, dst_ref=dst, send_sem=send_sem, recv_sem=recv_sem, device_id=(p, q), device_id_type=MESH
    )


def loop(lo, hi, fn):
    def step(i, carry):
        fn(i)
        return carry

    lax.fori_loop(lo, hi, step, 0)


def rows(ref, i, n=S):
    return ref.at[pl.ds(pl.multiple_of(i * n, n), n)]


def kernel(a_hbm, r_hbm, o_ref, a_ref, r_ref, vp, vc, low, pc, cbuf, nbuf, psum, abuf, rowbuf, rpart, wsl, wp, vrel, wrel,
           gterm, gs, gx, gram, mterm, ms, mx, mtot, stack, coef, yp, lhs, rhs,
           in_s, v_s, v_r, vf_s, vf_r, w_s, w_r, wf_s, wf_r, c1_s, c1_r, c2_s, c2_r, c3_s, c3_r, row_s, row_r, wr_s, wr_r,
           gx_s, gx_r, ga_s, ga_r, mx_s, mx_r, ma_s, ma_r):
    p = lax.axis_index("prow")
    q = lax.axis_index("pcol")
    y = p // Z
    z = lax.rem(p, Z)
    mate = q + 1 - 2 * lax.rem(q, 2)
    last_q = jnp.minimum(p, NQ - 1)
    get_r = pltpu.make_async_copy(r_hbm, r_ref, in_s.at[0])
    get_a = pltpu.make_async_copy(a_hbm, a_ref, in_s.at[1])
    get_r.start()
    get_a.start()

    def plane(d):
        return lax.rem(z + d + Z, Z)

    def some(n):
        ref = stack.at[pl.ds(0, n)]
        return ref, ref

    def sent(n, sem):
        copy_to(*some(n), sem, sem, p, mate).wait_send()

    def got(n, sem):
        copy_to(*some(n), sem, sem, p, mate).wait_recv()

    def if_any(n, fn, sem, most, least=0):
        if most == least:
            if most:
                fn(most * S, sem)
            return
        half = (least + most) // 2
        pl.when(n <= half)(lambda: if_any(n, fn, sem, half, least))
        pl.when(n > half)(lambda: if_any(n, fn, sem, most, half + 1))

    def not_me(j, fn):
        @pl.when(j != q)
        def _():
            fn(j)

    def source(k):
        return plane((0, -FAR, FAR)[k]), (5, 6, 5)[k]

    def targets(k, fn):
        t, n = source(k)

        def one(i):
            yy = lax.rem(i, 2)
            pp = yy * Z + plane(i // 2 - 2)
            fn(i, pp, t, pp > y * Z + t, (pp == p) & (t == q))

        loop(0, 2 * n, one)

    barrier = pltpu.get_barrier_semaphore()

    def greet(pp, qq):
        pl.semaphore_signal(barrier, inc=1, device_id=(pp, qq), device_id_type=MESH)

    for d in (FAR, -FAR):
        greet((1 - y) * Z + plane(d), q)
    for d in (FAR, -FAR, 3, 2, -2, 1, -1):
        greet(y * Z + plane(d), q)
    off = lax.rem(z - q + 7 + Z, Z) - 7
    step = jnp.where(off < -2, -FAR, jnp.where(off > 2, FAR, 0))
    from_z = lax.rem(q + step + Z, Z)
    for h in range(2):
        @pl.when(q + h * NQ < p)
        def _():
            def hello(j):
                @pl.when((h != y) | (from_z != z) | (j != q))
                def _():
                    greet(h * Z + from_z, j)

            loop(0, NQ, hello)

    loop(1, NQ, lambda d: greet(p, lax.rem(q + d, NQ)))
    loop(0, NQ, lambda j: greet((1 - y) * Z + z, j))
    fans = jnp.int32(0)
    for k in range(3):
        t, n = source(k)
        for i in range(2 * n):
            pp = (i % 2) * Z + plane(i // 2 - 2)
            fans += ((pp > y * Z + t) & ((pp != p) | (t != q))).astype(jnp.int32)

    get_r.wait()
    raw = r_ref[...]
    ii = lax.broadcasted_iota(jnp.int32, (T, T), 0)
    jj = lax.broadcasted_iota(jnp.int32, (T, T), 1)
    unit = jnp.where(ii > jj, raw, jnp.where(ii == jj, 1.0, 0.0))
    vp[...] = jnp.where(p == 0, 0.0, jnp.where(p == 1, unit, raw)).T
    gterm[...] = dot(vp[pl.ds(pl.multiple_of(q * S, S), S), :], vp[...], 1, 1)
    get_a.wait()
    for h in range(2):
        c = q + h * NQ

        @pl.when(c <= p)
        def _():
            tile = a_ref[:, h, :] * jnp.where(c < p, 1.0, 0.5)
            low[h] = tile
            pc[h] = dot(vp[...], tile)

        @pl.when(c == p)
        def _():
            vc[h] = vp[...]

    pl.semaphore_wait(barrier, 9 + 31 + fans)

    def first(src, rel, f_s, f_r):
        return [
            copy_to(src, rel.at[0], f_s, f_r.at[0], y * Z + plane(FAR), q),
            copy_to(src, rel.at[1], f_s, f_r.at[1], y * Z + plane(-FAR), q),
        ]

    def fan(k, src, dst, s_s, s_r):
        def send(i, pp, t, live, me):
            @pl.when(live & jnp.logical_not(me))
            def _():
                copy_to(src, dst, s_s, s_r.at[y], pp, t).start()

            @pl.when(live & me)
            def _():
                pltpu.make_async_copy(src, dst, s_r.at[y]).start()

        targets(k, send)

    v_mine = rows(vp, q)
    v_dst = rows(vc.at[y], q)
    w_dst = rhs.at[y, pl.ds(pl.multiple_of(T + q * S, S), S)]
    v_first = first(v_mine, vrel, vf_s, vf_r)
    for c in v_first:
        c.start()
    fan(0, v_mine, v_dst, v_s, v_r)

    def c1_copy(h, j):
        return copy_to(rows(pc.at[h], j), cbuf.at[y, q], c1_s.at[h], c1_r.at[y], h * Z + z, j)

    def c1_each(h, fn):
        def one(d):
            j = lax.rem(q + d, NQ)

            @pl.when((h != y) | (j != q))
            def _():
                fn(c1_copy(h, j))

        loop(0, NQ, one)

    for h in range(2):
        @pl.when(q + h * NQ <= p)
        def _():
            c1_each(h, lambda c: c.start())

            @pl.when(h == y)
            def _():
                cbuf[y, q] = pc[h, pl.ds(pl.multiple_of(q * S, S), S), :]


    def sum_far(term, parts, s, r):
        out = []
        for k, (d, yy) in enumerate(((FAR, y), (-FAR, y), (FAR, 1 - y), (-FAR, 1 - y), (0, 1 - y))):
            out.append(copy_to(rows(term, yy, H), parts.at[k], s, r.at[0], yy * Z + plane(d), q))
        return out

    def sum_far_end(term, buf, parts, r):
        got(5 * H, r.at[0])
        above = parts[1] + parts[3]
        buf[0] = (term[pl.ds(pl.multiple_of(y * H, H), H), :] + above) + (parts[0] + parts[2] + parts[4])
        buf[1] = above

    def sum_near(buf, parts, s, r):
        return [
            copy_to(buf.at[1 if k == 0 else 0], parts.at[5 + k], s, r.at[1], y * Z + plane(d), q)
            for k, d in enumerate((-3, -2, 2, -1, 1))
        ]

    def sum_near_end(buf, parts, r):
        got(5 * H, r.at[1])
        total = buf[0]
        for k in range(5):
            total += parts[5 + k]
        buf[2] = total

    def all_send(buf, dst, s, r):
        def one(d):
            i = lax.rem(y * NQ + q + d, 2 * NQ)
            copy_to(buf.at[2], rows(dst, 2 * q + y, H), s, r, i // NQ * Z + z, lax.rem(i, NQ)).start()

        loop(1, 2 * NQ, one)
        dst[pl.ds(pl.multiple_of((2 * q + y) * H, H), H), :] = buf[2]

    g_far = sum_far(gterm, gx, gx_s, gx_r)
    for c in g_far:
        c.start()

    def relay(k, rel, f_s, f_r, dst, s_s, s_r):
        copy_to(rel.at[k - 1], rel.at[k - 1], f_s, f_r.at[k - 1], p, q).wait_recv()
        fan(k, rel.at[k - 1], dst, s_s, s_r)

    for k in (1, 2):
        relay(k, vrel, vf_s, vf_r, v_dst, v_s, v_r)

    def group(n):
        off = jnp.where(n < 6, n + 3, jnp.where(n < 11, 3 - n, n - 13))
        k = jnp.where(off > 2, 1, jnp.where(off < -2, 2, 0))
        a = jnp.where(off > 2, FAR, jnp.where(off < -2, -FAR, 0))
        return plane(-off), k, a, off - a

    def c2_copy(n):
        i, k, a, b = group(n)
        return copy_to(cbuf.at[1, i], nbuf.at[k, b + 2], c2_s, c2_r.at[k], y * Z + plane(-b), q)

    def c2_each(fn):
        def one(n):
            i, k, a, b = group(n)

            @pl.when((y == 0) | (i <= z))
            def _():
                fn(n, i, b)

        loop(0, Z, one)

    def c2_send(n, i, b):
        @pl.when((y == 0) & (i <= z))
        def _():
            cbuf[1, i] += cbuf[0, i]

        @pl.when(b != 0)
        def _():
            c2_copy(n).start()

    own = (q <= z).astype(jnp.int32)
    if_any(z + 1 - own, got, c1_r.at[y], NQ)

    @pl.when(y == 0)
    def _():
        got(T, c1_r.at[1])

    c2_each(c2_send)

    def c3_copy(k):
        return copy_to(psum.at[k], abuf.at[k - 1], c3_s, c3_r, y * Z + source(k)[0], q)

    def c3_sum(k):
        t, n = source(k)
        psum[k] = jnp.zeros((S, T), f32)

        @pl.when((y == 0) | (t <= z))
        def _():
            psum[k] = cbuf[1, t]

        live = [((y == 0) | (t <= plane(i - 2))).astype(jnp.int32) for i in range(n) if i != 2]
        if_any(sum(live), got, c2_r.at[k], n - 1)

        def add(i):
            @pl.when((i != 2) & ((y == 0) | (t <= plane(i - 2))))
            def _():
                psum[k] += nbuf[k, i]

        loop(0, n, add)


    sum_far_end(gterm, gs, gx, gx_r)
    g_near = sum_near(gs, gx, gx_s, gx_r)
    for c in g_near:
        c.start()

    for h in range(2):
        @pl.when(q + h * NQ < p)
        def _():
            copy_to(vc.at[h], vc.at[h], v_s, v_r.at[h], p, q).wait_recv()

    @pl.when(q <= p)
    def _():
        rpart[...] = dot(vc[0], low[0], 1, 1)

    @pl.when(q + NQ <= p)
    def _():
        rpart[...] += dot(vc[1], low[1], 1, 1)

    def row_copy(j):
        return copy_to(rows(rpart, j), rowbuf.at[q], row_s, row_r, p, j)

    @pl.when(q <= p)
    def _():
        loop(1, NQ, lambda d: row_copy(lax.rem(q + d, NQ)).start())
        rowbuf[q] = rpart[pl.ds(pl.multiple_of(q * S, S), S), :]

    for k in (1, 2):
        c3_sum(k)
        c3_copy(k).start()

    sum_near_end(gs, gx, gx_r)
    all_send(gs, gram, ga_s, ga_r)
    c3_sum(0)

    wsl[...] = jnp.zeros((S, T), f32)

    others = last_q + 1 - (q <= last_q).astype(jnp.int32)
    if_any(others, got, row_r, NQ)

    def row_add(j):
        wsl[...] += rowbuf[j]

    loop(0, last_q + 1, row_add)
    mterm[...] = dot(wsl[...], vp[...], 1, 1)
    m_far = sum_far(mterm, mx, mx_s, mx_r)
    for c in m_far:
        c.start()

    got(2 * S, c3_r)
    wsl[...] += (psum[0] + abuf[0]) + abuf[1]
    w_first = first(wsl, wrel, wf_s, wf_r)
    for c in w_first:
        c.start()
    fan(0, wsl, w_dst, w_s, w_r)

    def wrow_copy(j):
        return copy_to(wsl, rows(wp, q), wr_s, wr_r, p, j)

    loop(0, last_q + 1, lambda j: not_me(j, lambda i: wrow_copy(i).start()))
    wp[pl.ds(pl.multiple_of(q * S, S), S), :] = wsl[...]

    if_any(fans, sent, v_s, 32)
    sent(2 * S, vf_s)
    for h in range(2):
        @pl.when((q + h * NQ <= p) & (h == y))
        def _():
            sent(T - S, c1_s.at[h])

        @pl.when((q + h * NQ <= p) & (h != y))
        def _():
            sent(T, c1_s.at[h])

    live = jnp.where(y == 0, Z, z + 1)
    for k in range(3):
        live -= ((y == 0) | (source(k)[0] <= z)).astype(jnp.int32)
    if_any(live, sent, c2_s, Z)
    sent(2 * S, c3_s)

    @pl.when(q <= p)
    def _():
        sent(T - S, row_s)

    sent(10 * H, gx_s)

    got(T - H, ga_r)
    diag = jnp.where(ii == jj, 0.5 * gram[...], 0.0)
    power = jnp.where(ii < jj, -gram[...], 0.0) / jnp.sum(diag, axis=1, keepdims=True)
    stack[0:T] = jnp.where(ii == jj, 1.0, power)
    stack[T:] = dot(power, power)

    def double(_):
        both = dot(stack[...], stack[T:])
        stack[0:T] += both[0:T]
        stack[T:] = both[T:]

    loop(0, 4, double)

    sum_far_end(mterm, ms, mx, mx_r)
    m_near = sum_near(ms, mx, mx_s, mx_r)
    for c in m_near:
        c.start()

    for k in (1, 2):
        relay(k, wrel, wf_s, wf_r, w_dst, w_s, w_r)

    loop(0, 2, double)
    coef[...] = (stack[0:T] + dot(stack[0:T], stack[T:])) / jnp.sum(diag, axis=0, keepdims=True)

    sum_near_end(ms, mx, mx_r)
    all_send(ms, mtot, ma_s, ma_r)
    yp[...] = dot(coef[...], vp[...])
    lhs[T:] = -yp[...]
    for h in range(2):
        @pl.when(q + h * NQ <= p)
        def _():
            rhs[h, 0:T] = dot(coef[...], vc[h])

    @pl.when(q <= p)
    def _():
        got(T - S, wr_r)
        lhs[0:T] = -wp[...]

    for h in range(2):
        c = q + h * NQ

        @pl.when(c < p)
        def _():
            copy_to(rhs.at[h, pl.ds(T, T)], rhs.at[h, pl.ds(T, T)], w_s, w_r.at[h], p, q).wait_recv()

        @pl.when(c == p)
        def _():
            rhs[h, T:] = wp[...]

        @pl.when(c <= p)
        def _():
            tile = a_ref[:, h, :]
            sym = jnp.where(c < p, tile, 0.5 * (tile + tile.T))
            low[h] = sym + dot(lhs[...], rhs[h], 0, 0)

    if_any(fans, sent, w_s, 32)
    sent(2 * S, wf_s)
    if_any(others, sent, wr_s, NQ)
    sent(T - H, ga_s)
    sent(10 * H, mx_s)

    got(T - H, ma_r)
    wp[...] = dot(mtot[...] + mtot[...].T, yp[...])
    for h in range(2):
        c = q + h * NQ

        @pl.when(c <= p)
        def _():
            o_ref[:, h, :] = low[h] + dot(wp[...], rhs[h, 0:T], 0, 0)

        @pl.when(c > p)
        def _():
            o_ref[:, h, :] = jnp.zeros((T, T), f32)

    sent(T - H, ma_s)


def body(matrix, reflectors):
    vmem = lambda *shape: pltpu.VMEM(shape, f32)
    dma = lambda *shape: pltpu.SemaphoreType.DMA(shape)
    one = pltpu.SemaphoreType.DMA
    out = pl.pallas_call(
        kernel,
        out_shape=jax.ShapeDtypeStruct((T, 2, T), f32),
        in_specs=[pl.BlockSpec(memory_space=pltpu.HBM)] * 2,
        out_specs=pl.BlockSpec(memory_space=pltpu.VMEM),
        scratch_shapes=[
            vmem(T, 2, T), vmem(T, T),
            vmem(T, T), vmem(2, T, T), vmem(2, T, T), vmem(2, T, T),
            vmem(2, NQ, S, T), vmem(3, 6, S, T), vmem(3, S, T), vmem(2, S, T), vmem(NQ, S, T),
            vmem(T, T), vmem(S, T), vmem(T, T), vmem(2, S, T), vmem(2, S, T),
            vmem(S, T), vmem(3, H, T), vmem(10, H, T), vmem(T, T),
            vmem(S, T), vmem(3, H, T), vmem(10, H, T), vmem(T, T),
            vmem(2 * T, T), vmem(T, T), vmem(T, T), vmem(2 * T, T), vmem(2, 2 * T, T),
            dma(2), one, dma(2), one, dma(2), one, dma(2), one, dma(2),
            dma(2), dma(2), one, dma(3), one, one, one, one, one, one,
            one, dma(2), one, one, one, dma(2), one, one,
        ],
        compiler_params=pltpu.CompilerParams(collective_id=0, has_side_effects=True, vmem_limit_bytes=53 * 2**20),
        cost_estimate=pl.CostEstimate(flops=34 * 2 * T**3, bytes_accessed=5 * T * T * 4, transcendentals=0),
    )(matrix.reshape(T, 2, T), reflectors.reshape(T, T))
    return out.reshape(matrix.shape)


def solution(mesh):
    placed = (P(None, "prow", None, "pcol"), P(None, "prow", None))
    return jax.shard_map(
        body, mesh=mesh, in_specs=placed, out_specs=P(None, "prow", None, "pcol"), check_vma=False
    )
```

```python
import jax
import jax.numpy as jnp
from jax import lax
from jax.experimental import pallas as pl
from jax.experimental.pallas import tpu as pltpu
from jax.sharding import PartitionSpec as P

MESH = pl.DeviceIdType.MESH
f32 = jnp.float32
NP, NQ, T, S = 32, 16, 256, 16
H = S // 2
Z = 16
FAR = 5


def dot(a, b, ca=1, cb=0):
    return lax.dot_general(a, b, (((ca,), (cb,)), ((), ())), precision=lax.Precision.HIGHEST, preferred_element_type=f32)


def copy_to(src, dst, send_sem, recv_sem, p, q):
    return pltpu.make_async_remote_copy(
        src_ref=src, dst_ref=dst, send_sem=send_sem, recv_sem=recv_sem, device_id=(p, q), device_id_type=MESH
    )


def loop(lo, hi, fn):
    def step(i, carry):
        fn(i)
        return carry

    lax.fori_loop(lo, hi, step, 0)


def rows(ref, i, n=S):
    return ref.at[pl.ds(pl.multiple_of(i * n, n), n)]


def kernel(a_hbm, r_hbm, o_ref, a_ref, r_ref, vp, vc, low, pc, cbuf, nbuf, psum, abuf, rowbuf, rpart, wsl, wp, vrel, wrel,
           gterm, gs, gx, gram, mterm, ms, mx, mtot, stack, coef, yp, lhs, rhs,
           in_s, v_s, v_r, vf_s, vf_r, w_s, w_r, wf_s, wf_r, c1_s, c1_r, c2_s, c2_r, c3_s, c3_r, row_s, row_r, wr_s, wr_r,
           gx_s, gx_r, ga_s, ga_r, mx_s, mx_r, ma_s, ma_r):
    p = lax.axis_index("prow")
    q = lax.axis_index("pcol")
    y = p // Z
    z = lax.rem(p, Z)
    mate = q + 1 - 2 * lax.rem(q, 2)
    last_q = jnp.minimum(p, NQ - 1)
    get_r = pltpu.make_async_copy(r_hbm, r_ref, in_s.at[0])
    get_a = pltpu.make_async_copy(a_hbm, a_ref, in_s.at[1])
    get_r.start()
    get_a.start()

    def plane(d):
        return lax.rem(z + d + Z, Z)

    def some(n):
        ref = stack.at[pl.ds(0, n)]
        return ref, ref

    def sent(n, sem):
        copy_to(*some(n), sem, sem, p, mate).wait_send()

    def got(n, sem):
        copy_to(*some(n), sem, sem, p, mate).wait_recv()

    def if_any(n, fn, sem, most, least=0):
        if most == least:
            if most:
                fn(most * S, sem)
            return
        half = (least + most) // 2
        pl.when(n <= half)(lambda: if_any(n, fn, sem, half, least))
        pl.when(n > half)(lambda: if_any(n, fn, sem, most, half + 1))

    def not_me(j, fn):
        @pl.when(j != q)
        def _():
            fn(j)

    def source(k):
        return plane((0, -FAR, FAR)[k]), (5, 6, 5)[k]

    def targets(k, fn):
        t, n = source(k)

        def one(i):
            yy = lax.rem(i, 2)
            pp = yy * Z + plane(i // 2 - 2)
            fn(i, pp, t, pp > y * Z + t, (pp == p) & (t == q))

        loop(0, 2 * n, one)

    barrier = pltpu.get_barrier_semaphore()

    def greet(pp, qq):
        pl.semaphore_signal(barrier, inc=1, device_id=(pp, qq), device_id_type=MESH)

    for d in (FAR, -FAR):
        greet((1 - y) * Z + plane(d), q)
    for d in (FAR, -FAR, 3, 2, -2, 1, -1):
        greet(y * Z + plane(d), q)
    off = lax.rem(z - q + 7 + Z, Z) - 7
    step = jnp.where(off < -2, -FAR, jnp.where(off > 2, FAR, 0))
    from_z = lax.rem(q + step + Z, Z)
    for h in range(2):
        @pl.when(q + h * NQ < p)
        def _():
            def hello(j):
                @pl.when((h != y) | (from_z != z) | (j != q))
                def _():
                    greet(h * Z + from_z, j)

            loop(0, NQ, hello)

    loop(1, NQ, lambda d: greet(p, lax.rem(q + d, NQ)))
    loop(0, NQ, lambda j: greet((1 - y) * Z + z, j))
    fans = jnp.int32(0)
    for k in range(3):
        t, n = source(k)
        for i in range(2 * n):
            pp = (i % 2) * Z + plane(i // 2 - 2)
            fans += ((pp > y * Z + t) & ((pp != p) | (t != q))).astype(jnp.int32)

    get_r.wait()
    raw = r_ref[...]
    ii = lax.broadcasted_iota(jnp.int32, (T, T), 0)
    jj = lax.broadcasted_iota(jnp.int32, (T, T), 1)
    unit = jnp.where(ii > jj, raw, jnp.where(ii == jj, 1.0, 0.0))
    vp[...] = jnp.where(p == 0, 0.0, jnp.where(p == 1, unit, raw)).T

    pl.semaphore_wait(barrier, 9 + 31 + fans)

    def first(src, rel, f_s, f_r):
        return [
            copy_to(src, rel.at[0], f_s, f_r.at[0], y * Z + plane(FAR), q),
            copy_to(src, rel.at[1], f_s, f_r.at[1], y * Z + plane(-FAR), q),
        ]

    def fan(k, src, dst, s_s, s_r):
        def send(i, pp, t, live, me):
            @pl.when(live & jnp.logical_not(me))
            def _():
                copy_to(src, dst, s_s, s_r.at[y], pp, t).start()

            @pl.when(live & me)
            def _():
                pltpu.make_async_copy(src, dst, s_r.at[y]).start()

        targets(k, send)

    v_mine = rows(vp, q)
    v_dst = rows(vc.at[y], q)
    w_dst = rhs.at[y, pl.ds(pl.multiple_of(T + q * S, S), S)]
    v_first = first(v_mine, vrel, vf_s, vf_r)
    for c in v_first:
        c.start()
    fan(0, v_mine, v_dst, v_s, v_r)

    gterm[...] = dot(vp[pl.ds(pl.multiple_of(q * S, S), S), :], vp[...], 1, 1)
    get_a.wait()
    for h in range(2):
        c = q + h * NQ

        @pl.when(c <= p)
        def _():
            tile = a_ref[:, h, :] * jnp.where(c < p, 1.0, 0.5)
            low[h] = tile
            pc[h] = dot(vp[...], tile)

        @pl.when(c == p)
        def _():
            vc[h] = vp[...]

    def c1_copy(h, j):
        return copy_to(rows(pc.at[h], j), cbuf.at[y, q], c1_s.at[h], c1_r.at[y], h * Z + z, j)

    def c1_each(h, fn):
        def one(d):
            j = lax.rem(q + d, NQ)

            @pl.when((h != y) | (j != q))
            def _():
                fn(c1_copy(h, j))

        loop(0, NQ, one)

    for h in range(2):
        @pl.when(q + h * NQ <= p)
        def _():
            c1_each(h, lambda c: c.start())

            @pl.when(h == y)
            def _():
                cbuf[y, q] = pc[h, pl.ds(pl.multiple_of(q * S, S), S), :]


    def sum_far(term, parts, s, r):
        out = []
        for k, (d, yy) in enumerate(((FAR, y), (-FAR, y), (FAR, 1 - y), (-FAR, 1 - y), (0, 1 - y))):
            out.append(copy_to(rows(term, yy, H), parts.at[k], s, r.at[0], yy * Z + plane(d), q))
        return out

    def sum_far_end(term, buf, parts, r):
        got(5 * H, r.at[0])
        above = parts[1] + parts[3]
        buf[0] = (term[pl.ds(pl.multiple_of(y * H, H), H), :] + above) + (parts[0] + parts[2] + parts[4])
        buf[1] = above

    def sum_near(buf, parts, s, r):
        return [
            copy_to(buf.at[1 if k == 0 else 0], parts.at[5 + k], s, r.at[1], y * Z + plane(d), q)
            for k, d in enumerate((-3, -2, 2, -1, 1))
        ]

    def sum_near_end(buf, parts, r):
        got(5 * H, r.at[1])
        total = buf[0]
        for k in range(5):
            total += parts[5 + k]
        buf[2] = total

    def all_send(buf, dst, s, r):
        def one(d):
            i = lax.rem(y * NQ + q + d, 2 * NQ)
            copy_to(buf.at[2], rows(dst, 2 * q + y, H), s, r, i // NQ * Z + z, lax.rem(i, NQ)).start()

        loop(1, 2 * NQ, one)
        dst[pl.ds(pl.multiple_of((2 * q + y) * H, H), H), :] = buf[2]

    g_far = sum_far(gterm, gx, gx_s, gx_r)
    for c in g_far:
        c.start()

    def relay(k, rel, f_s, f_r, dst, s_s, s_r):
        copy_to(rel.at[k - 1], rel.at[k - 1], f_s, f_r.at[k - 1], p, q).wait_recv()
        fan(k, rel.at[k - 1], dst, s_s, s_r)

    for k in (1, 2):
        relay(k, vrel, vf_s, vf_r, v_dst, v_s, v_r)

    def group(n):
        off = jnp.where(n < 6, n + 3, jnp.where(n < 11, 3 - n, n - 13))
        k = jnp.where(off > 2, 1, jnp.where(off < -2, 2, 0))
        a = jnp.where(off > 2, FAR, jnp.where(off < -2, -FAR, 0))
        return plane(-off), k, a, off - a

    def c2_copy(n):
        i, k, a, b = group(n)
        return copy_to(cbuf.at[1, i], nbuf.at[k, b + 2], c2_s, c2_r.at[k], y * Z + plane(-b), q)

    def c2_each(fn):
        def one(n):
            i, k, a, b = group(n)

            @pl.when((y == 0) | (i <= z))
            def _():
                fn(n, i, b)

        loop(0, Z, one)

    def c2_send(n, i, b):
        @pl.when((y == 0) & (i <= z))
        def _():
            cbuf[1, i] += cbuf[0, i]

        @pl.when(b != 0)
        def _():
            c2_copy(n).start()

    own = (q <= z).astype(jnp.int32)
    if_any(z + 1 - own, got, c1_r.at[y], NQ)

    @pl.when(y == 0)
    def _():
        got(T, c1_r.at[1])

    c2_each(c2_send)

    def c3_copy(k):
        return copy_to(psum.at[k], abuf.at[k - 1], c3_s, c3_r, y * Z + source(k)[0], q)

    def c3_sum(k):
        t, n = source(k)
        psum[k] = jnp.zeros((S, T), f32)

        @pl.when((y == 0) | (t <= z))
        def _():
            psum[k] = cbuf[1, t]

        live = [((y == 0) | (t <= plane(i - 2))).astype(jnp.int32) for i in range(n) if i != 2]
        if_any(sum(live), got, c2_r.at[k], n - 1)

        def add(i):
            @pl.when((i != 2) & ((y == 0) | (t <= plane(i - 2))))
            def _():
                psum[k] += nbuf[k, i]

        loop(0, n, add)


    sum_far_end(gterm, gs, gx, gx_r)
    g_near = sum_near(gs, gx, gx_s, gx_r)
    for c in g_near:
        c.start()

    for h in range(2):
        @pl.when(q + h * NQ < p)
        def _():
            copy_to(vc.at[h], vc.at[h], v_s, v_r.at[h], p, q).wait_recv()

    @pl.when(q <= p)
    def _():
        rpart[...] = dot(vc[0], low[0], 1, 1)

    @pl.when(q + NQ <= p)
    def _():
        rpart[...] += dot(vc[1], low[1], 1, 1)

    def row_copy(j):
        return copy_to(rows(rpart, j), rowbuf.at[q], row_s, row_r, p, j)

    @pl.when(q <= p)
    def _():
        loop(1, NQ, lambda d: row_copy(lax.rem(q + d, NQ)).start())
        rowbuf[q] = rpart[pl.ds(pl.multiple_of(q * S, S), S), :]

    for k in (1, 2):
        c3_sum(k)
        c3_copy(k).start()

    sum_near_end(gs, gx, gx_r)
    all_send(gs, gram, ga_s, ga_r)
    c3_sum(0)

    wsl[...] = jnp.zeros((S, T), f32)

    others = last_q + 1 - (q <= last_q).astype(jnp.int32)
    if_any(others, got, row_r, NQ)

    def row_add(j):
        wsl[...] += rowbuf[j]

    loop(0, last_q + 1, row_add)
    mterm[...] = dot(wsl[...], vp[...], 1, 1)
    m_far = sum_far(mterm, mx, mx_s, mx_r)
    for c in m_far:
        c.start()

    got(2 * S, c3_r)
    wsl[...] += (psum[0] + abuf[0]) + abuf[1]
    w_first = first(wsl, wrel, wf_s, wf_r)
    for c in w_first:
        c.start()
    fan(0, wsl, w_dst, w_s, w_r)

    def wrow_copy(j):
        return copy_to(wsl, rows(wp, q), wr_s, wr_r, p, j)

    loop(0, last_q + 1, lambda j: not_me(j, lambda i: wrow_copy(i).start()))
    wp[pl.ds(pl.multiple_of(q * S, S), S), :] = wsl[...]

    if_any(fans, sent, v_s, 32)
    sent(2 * S, vf_s)
    for h in range(2):
        @pl.when((q + h * NQ <= p) & (h == y))
        def _():
            sent(T - S, c1_s.at[h])

        @pl.when((q + h * NQ <= p) & (h != y))
        def _():
            sent(T, c1_s.at[h])

    live = jnp.where(y == 0, Z, z + 1)
    for k in range(3):
        live -= ((y == 0) | (source(k)[0] <= z)).astype(jnp.int32)
    if_any(live, sent, c2_s, Z)
    sent(2 * S, c3_s)

    @pl.when(q <= p)
    def _():
        sent(T - S, row_s)

    sent(10 * H, gx_s)

    got(T - H, ga_r)
    diag = jnp.where(ii == jj, 0.5 * gram[...], 0.0)
    power = jnp.where(ii < jj, -gram[...], 0.0) / jnp.sum(diag, axis=1, keepdims=True)
    stack[0:T] = jnp.where(ii == jj, 1.0, power)
    stack[T:] = dot(power, power)

    def double(_):
        both = dot(stack[...], stack[T:])
        stack[0:T] += both[0:T]
        stack[T:] = both[T:]

    loop(0, 4, double)

    sum_far_end(mterm, ms, mx, mx_r)
    m_near = sum_near(ms, mx, mx_s, mx_r)
    for c in m_near:
        c.start()

    for k in (1, 2):
        relay(k, wrel, wf_s, wf_r, w_dst, w_s, w_r)

    loop(0, 2, double)
    coef[...] = (stack[0:T] + dot(stack[0:T], stack[T:])) / jnp.sum(diag, axis=0, keepdims=True)

    sum_near_end(ms, mx, mx_r)
    all_send(ms, mtot, ma_s, ma_r)
    yp[...] = dot(coef[...], vp[...])
    lhs[T:] = -yp[...]
    for h in range(2):
        @pl.when(q + h * NQ <= p)
        def _():
            rhs[h, 0:T] = dot(coef[...], vc[h])

    @pl.when(q <= p)
    def _():
        got(T - S, wr_r)
        lhs[0:T] = -wp[...]

    for h in range(2):
        c = q + h * NQ

        @pl.when(c < p)
        def _():
            copy_to(rhs.at[h, pl.ds(T, T)], rhs.at[h, pl.ds(T, T)], w_s, w_r.at[h], p, q).wait_recv()

        @pl.when(c == p)
        def _():
            rhs[h, T:] = wp[...]

        @pl.when(c <= p)
        def _():
            tile = a_ref[:, h, :]
            sym = jnp.where(c < p, tile, 0.5 * (tile + tile.T))
            low[h] = sym + dot(lhs[...], rhs[h], 0, 0)

    if_any(fans, sent, w_s, 32)
    sent(2 * S, wf_s)
    if_any(others, sent, wr_s, NQ)
    sent(T - H, ga_s)
    sent(10 * H, mx_s)

    got(T - H, ma_r)
    wp[...] = dot(mtot[...] + mtot[...].T, yp[...])
    for h in range(2):
        c = q + h * NQ

        @pl.when(c <= p)
        def _():
            o_ref[:, h, :] = low[h] + dot(wp[...], rhs[h, 0:T], 0, 0)

        @pl.when(c > p)
        def _():
            o_ref[:, h, :] = jnp.zeros((T, T), f32)

    sent(T - H, ma_s)


def body(matrix, reflectors):
    vmem = lambda *shape: pltpu.VMEM(shape, f32)
    dma = lambda *shape: pltpu.SemaphoreType.DMA(shape)
    one = pltpu.SemaphoreType.DMA
    out = pl.pallas_call(
        kernel,
        out_shape=jax.ShapeDtypeStruct((T, 2, T), f32),
        in_specs=[pl.BlockSpec(memory_space=pltpu.HBM)] * 2,
        out_specs=pl.BlockSpec(memory_space=pltpu.VMEM),
        scratch_shapes=[
            vmem(T, 2, T), vmem(T, T),
            vmem(T, T), vmem(2, T, T), vmem(2, T, T), vmem(2, T, T),
            vmem(2, NQ, S, T), vmem(3, 6, S, T), vmem(3, S, T), vmem(2, S, T), vmem(NQ, S, T),
            vmem(T, T), vmem(S, T), vmem(T, T), vmem(2, S, T), vmem(2, S, T),
            vmem(S, T), vmem(3, H, T), vmem(10, H, T), vmem(T, T),
            vmem(S, T), vmem(3, H, T), vmem(10, H, T), vmem(T, T),
            vmem(2 * T, T), vmem(T, T), vmem(T, T), vmem(2 * T, T), vmem(2, 2 * T, T),
            dma(2), one, dma(2), one, dma(2), one, dma(2), one, dma(2),
            dma(2), dma(2), one, dma(3), one, one, one, one, one, one,
            one, dma(2), one, one, one, dma(2), one, one,
        ],
        compiler_params=pltpu.CompilerParams(collective_id=0, has_side_effects=True, vmem_limit_bytes=53 * 2**20),
        cost_estimate=pl.CostEstimate(flops=34 * 2 * T**3, bytes_accessed=5 * T * T * 4, transcendentals=0),
    )(matrix.reshape(T, 2, T), reflectors.reshape(T, T))
    return out.reshape(matrix.shape)


def solution(mesh):
    placed = (P(None, "prow", None, "pcol"), P(None, "prow", None))
    return jax.shard_map(
        body, mesh=mesh, in_specs=placed, out_specs=P(None, "prow", None, "pcol"), check_vma=False
    )
```

```python
import jax
import jax.numpy as jnp
from jax import lax
from jax.experimental import pallas as pl
from jax.experimental.pallas import tpu as pltpu
from jax.sharding import PartitionSpec as P

MESH = pl.DeviceIdType.MESH
f32 = jnp.float32
NP, NQ, T, S = 32, 16, 256, 16
H = S // 2
Z = 16
FAR = 5


def dot(a, b, ca=1, cb=0):
    return lax.dot_general(a, b, (((ca,), (cb,)), ((), ())), precision=lax.Precision.HIGHEST, preferred_element_type=f32)


def copy_to(src, dst, send_sem, recv_sem, p, q):
    return pltpu.make_async_remote_copy(
        src_ref=src, dst_ref=dst, send_sem=send_sem, recv_sem=recv_sem, device_id=(p, q), device_id_type=MESH
    )


def loop(lo, hi, fn):
    def step(i, carry):
        fn(i)
        return carry

    lax.fori_loop(lo, hi, step, 0)


def rows(ref, i, n=S):
    return ref.at[pl.ds(pl.multiple_of(i * n, n), n)]


def kernel(a_hbm, r_hbm, o_ref, a_ref, r_ref, vp, vc, low, pc, cbuf, nbuf, psum, abuf, rowbuf, rpart, wsl, wp, vrel, wrel,
           gterm, gs, gx, gram, mterm, ms, mx, mtot, stack, coef, yp, lhs, rhs,
           in_s, v_s, v_r, vf_s, vf_r, w_s, w_r, wf_s, wf_r, c1_s, c1_r, c2_s, c2_r, c3_s, c3_r, row_s, row_r, wr_s, wr_r,
           gx_s, gx_r, ga_s, ga_r, mx_s, mx_r, ma_s, ma_r):
    p = lax.axis_index("prow")
    q = lax.axis_index("pcol")
    y = p // Z
    z = lax.rem(p, Z)
    mate = q + 1 - 2 * lax.rem(q, 2)
    last_q = jnp.minimum(p, NQ - 1)
    get_r = pltpu.make_async_copy(r_hbm, r_ref, in_s.at[0])
    get_a = pltpu.make_async_copy(a_hbm, a_ref, in_s.at[1])
    get_r.start()
    get_a.start()

    def plane(d):
        return lax.rem(z + d + Z, Z)

    def some(n):
        ref = stack.at[pl.ds(0, n)]
        return ref, ref

    def sent(n, sem):
        copy_to(*some(n), sem, sem, p, mate).wait_send()

    def got(n, sem):
        copy_to(*some(n), sem, sem, p, mate).wait_recv()

    def if_any(n, fn, sem, most, least=0):
        if most == least:
            if most:
                fn(most * S, sem)
            return
        half = (least + most) // 2
        pl.when(n <= half)(lambda: if_any(n, fn, sem, half, least))
        pl.when(n > half)(lambda: if_any(n, fn, sem, most, half + 1))

    def not_me(j, fn):
        @pl.when(j != q)
        def _():
            fn(j)

    def source(k):
        return plane((0, -FAR, FAR)[k]), (5, 6, 5)[k]

    def targets(k, fn):
        t, n = source(k)

        def one(i):
            yy = lax.rem(i, 2)
            pp = yy * Z + plane(i // 2 - 2)
            fn(i, pp, t, pp > y * Z + t, (pp == p) & (t == q))

        loop(0, 2 * n, one)

    barrier = pltpu.get_barrier_semaphore()

    def greet(pp, qq):
        pl.semaphore_signal(barrier, inc=1, device_id=(pp, qq), device_id_type=MESH)

    for d in (FAR, -FAR):
        greet((1 - y) * Z + plane(d), q)
    for d in (FAR, -FAR, 3, 2, -2, 1, -1):
        greet(y * Z + plane(d), q)
    off = lax.rem(z - q + 7 + Z, Z) - 7
    step = jnp.where(off < -2, -FAR, jnp.where(off > 2, FAR, 0))
    from_z = lax.rem(q + step + Z, Z)
    for h in range(2):
        @pl.when(q + h * NQ < p)
        def _():
            def hello(j):
                @pl.when((h != y) | (from_z != z) | (j != q))
                def _():
                    greet(h * Z + from_z, j)

            loop(0, NQ, hello)

    loop(1, NQ, lambda d: greet(p, lax.rem(q + d, NQ)))
    loop(0, NQ, lambda j: greet((1 - y) * Z + z, j))
    fans = jnp.int32(0)
    for k in range(3):
        t, n = source(k)
        for i in range(2 * n):
            pp = (i % 2) * Z + plane(i // 2 - 2)
            fans += ((pp > y * Z + t) & ((pp != p) | (t != q))).astype(jnp.int32)

    get_r.wait()
    raw = r_ref[...]
    ii = lax.broadcasted_iota(jnp.int32, (T, T), 0)
    jj = lax.broadcasted_iota(jnp.int32, (T, T), 1)
    unit = jnp.where(ii > jj, raw, jnp.where(ii == jj, 1.0, 0.0))
    vp[...] = jnp.where(p == 0, 0.0, jnp.where(p == 1, unit, raw)).T

    pl.semaphore_wait(barrier, 9 + 31 + fans)

    def first(src, rel, f_s, f_r):
        return [
            copy_to(src, rel.at[0], f_s, f_r.at[0], y * Z + plane(FAR), q),
            copy_to(src, rel.at[1], f_s, f_r.at[1], y * Z + plane(-FAR), q),
        ]

    def fan(k, src, dst, s_s, s_r):
        def send(i, pp, t, live, me):
            @pl.when(live & jnp.logical_not(me))
            def _():
                copy_to(src, dst, s_s, s_r.at[y], pp, t).start()

            @pl.when(live & me)
            def _():
                pltpu.make_async_copy(src, dst, s_r.at[y]).start()

        targets(k, send)

    v_mine = rows(vp, q)
    v_dst = rows(vc.at[y], q)
    w_dst = rhs.at[y, pl.ds(pl.multiple_of(T + q * S, S), S)]
    v_first = first(v_mine, vrel, vf_s, vf_r)
    for c in v_first:
        c.start()
    fan(0, v_mine, v_dst, v_s, v_r)

    gterm[...] = dot(vp[pl.ds(pl.multiple_of(q * S, S), S), :], vp[...], 1, 1)
    get_a.wait()
    for h in range(2):
        c = q + h * NQ

        @pl.when(c <= p)
        def _():
            tile = a_ref[:, h, :] * jnp.where(c < p, 1.0, 0.5)
            low[h] = tile
            pc[h] = dot(vp[...], tile)

        @pl.when(c == p)
        def _():
            vc[h] = vp[...]

    def c1_copy(h, j):
        return copy_to(rows(pc.at[h], j), cbuf.at[y, q], c1_s.at[h], c1_r.at[y], h * Z + z, j)

    def c1_each(h, fn):
        def one(d):
            j = lax.rem(q + d, NQ)

            @pl.when((h != y) | (j != q))
            def _():
                fn(c1_copy(h, j))

        loop(0, NQ, one)

    for h in range(2):
        @pl.when(q + h * NQ <= p)
        def _():
            c1_each(h, lambda c: c.start())

            @pl.when(h == y)
            def _():
                cbuf[y, q] = pc[h, pl.ds(pl.multiple_of(q * S, S), S), :]


    def sum_far(term, parts, s, r):
        out = []
        for k, (d, yy) in enumerate(((FAR, y), (-FAR, y), (FAR, 1 - y), (-FAR, 1 - y), (0, 1 - y))):
            out.append(copy_to(rows(term, yy, H), parts.at[k], s, r.at[0], yy * Z + plane(d), q))
        return out

    def sum_far_end(term, buf, parts, r):
        got(5 * H, r.at[0])
        above = parts[1] + parts[3]
        buf[0] = (term[pl.ds(pl.multiple_of(y * H, H), H), :] + above) + (parts[0] + parts[2] + parts[4])
        buf[1] = above

    def sum_near(buf, parts, s, r):
        return [
            copy_to(buf.at[1 if k == 0 else 0], parts.at[5 + k], s, r.at[1], y * Z + plane(d), q)
            for k, d in enumerate((-3, -2, 2, -1, 1))
        ]

    def sum_near_end(buf, parts, r):
        got(5 * H, r.at[1])
        total = buf[0]
        for k in range(5):
            total += parts[5 + k]
        buf[2] = total

    def all_send(buf, dst, s, r):
        def one(d):
            i = lax.rem(y * NQ + q + d, 2 * NQ)
            copy_to(buf.at[2], rows(dst, 2 * q + y, H), s, r, i // NQ * Z + z, lax.rem(i, NQ)).start()

        for d in range(1, 2 * NQ):
            one(d)
        dst[pl.ds(pl.multiple_of((2 * q + y) * H, H), H), :] = buf[2]

    g_far = sum_far(gterm, gx, gx_s, gx_r)
    for c in g_far:
        c.start()

    def relay(k, rel, f_s, f_r, dst, s_s, s_r):
        copy_to(rel.at[k - 1], rel.at[k - 1], f_s, f_r.at[k - 1], p, q).wait_recv()
        fan(k, rel.at[k - 1], dst, s_s, s_r)

    for k in (1, 2):
        relay(k, vrel, vf_s, vf_r, v_dst, v_s, v_r)

    def group(n):
        off = jnp.where(n < 6, n + 3, jnp.where(n < 11, 3 - n, n - 13))
        k = jnp.where(off > 2, 1, jnp.where(off < -2, 2, 0))
        a = jnp.where(off > 2, FAR, jnp.where(off < -2, -FAR, 0))
        return plane(-off), k, a, off - a

    def c2_copy(n):
        i, k, a, b = group(n)
        return copy_to(cbuf.at[1, i], nbuf.at[k, b + 2], c2_s, c2_r.at[k], y * Z + plane(-b), q)

    def c2_each(fn):
        def one(n):
            i, k, a, b = group(n)

            @pl.when((y == 0) | (i <= z))
            def _():
                fn(n, i, b)

        loop(0, Z, one)

    def c2_send(n, i, b):
        @pl.when((y == 0) & (i <= z))
        def _():
            cbuf[1, i] += cbuf[0, i]

        @pl.when(b != 0)
        def _():
            c2_copy(n).start()

    own = (q <= z).astype(jnp.int32)
    if_any(z + 1 - own, got, c1_r.at[y], NQ)

    @pl.when(y == 0)
    def _():
        got(T, c1_r.at[1])

    c2_each(c2_send)

    def c3_copy(k):
        return copy_to(psum.at[k], abuf.at[k - 1], c3_s, c3_r, y * Z + source(k)[0], q)

    def c3_sum(k):
        t, n = source(k)
        psum[k] = jnp.zeros((S, T), f32)

        @pl.when((y == 0) | (t <= z))
        def _():
            psum[k] = cbuf[1, t]

        live = [((y == 0) | (t <= plane(i - 2))).astype(jnp.int32) for i in range(n) if i != 2]
        if_any(sum(live), got, c2_r.at[k], n - 1)

        def add(i):
            @pl.when((i != 2) & ((y == 0) | (t <= plane(i - 2))))
            def _():
                psum[k] += nbuf[k, i]

        loop(0, n, add)


    sum_far_end(gterm, gs, gx, gx_r)
    g_near = sum_near(gs, gx, gx_s, gx_r)
    for c in g_near:
        c.start()

    for h in range(2):
        @pl.when(q + h * NQ < p)
        def _():
            copy_to(vc.at[h], vc.at[h], v_s, v_r.at[h], p, q).wait_recv()

    @pl.when(q <= p)
    def _():
        rpart[...] = dot(vc[0], low[0], 1, 1)

    @pl.when(q + NQ <= p)
    def _():
        rpart[...] += dot(vc[1], low[1], 1, 1)

    def row_copy(j):
        return copy_to(rows(rpart, j), rowbuf.at[q], row_s, row_r, p, j)

    @pl.when(q <= p)
    def _():
        loop(1, NQ, lambda d: row_copy(lax.rem(q + d, NQ)).start())
        rowbuf[q] = rpart[pl.ds(pl.multiple_of(q * S, S), S), :]

    for k in (1, 2):
        c3_sum(k)
        c3_copy(k).start()

    sum_near_end(gs, gx, gx_r)
    all_send(gs, gram, ga_s, ga_r)
    c3_sum(0)

    wsl[...] = jnp.zeros((S, T), f32)

    others = last_q + 1 - (q <= last_q).astype(jnp.int32)
    if_any(others, got, row_r, NQ)

    def row_add(j):
        wsl[...] += rowbuf[j]

    loop(0, last_q + 1, row_add)
    mterm[...] = dot(wsl[...], vp[...], 1, 1)
    m_far = sum_far(mterm, mx, mx_s, mx_r)
    for c in m_far:
        c.start()

    got(2 * S, c3_r)
    wsl[...] += (psum[0] + abuf[0]) + abuf[1]
    w_first = first(wsl, wrel, wf_s, wf_r)
    for c in w_first:
        c.start()
    fan(0, wsl, w_dst, w_s, w_r)

    def wrow_copy(j):
        return copy_to(wsl, rows(wp, q), wr_s, wr_r, p, j)

    loop(0, last_q + 1, lambda j: not_me(j, lambda i: wrow_copy(i).start()))
    wp[pl.ds(pl.multiple_of(q * S, S), S), :] = wsl[...]

    if_any(fans, sent, v_s, 32)
    sent(2 * S, vf_s)
    for h in range(2):
        @pl.when((q + h * NQ <= p) & (h == y))
        def _():
            sent(T - S, c1_s.at[h])

        @pl.when((q + h * NQ <= p) & (h != y))
        def _():
            sent(T, c1_s.at[h])

    live = jnp.where(y == 0, Z, z + 1)
    for k in range(3):
        live -= ((y == 0) | (source(k)[0] <= z)).astype(jnp.int32)
    if_any(live, sent, c2_s, Z)
    sent(2 * S, c3_s)

    @pl.when(q <= p)
    def _():
        sent(T - S, row_s)

    sent(10 * H, gx_s)

    got(T - H, ga_r)
    diag = jnp.where(ii == jj, 0.5 * gram[...], 0.0)
    power = jnp.where(ii < jj, -gram[...], 0.0) / jnp.sum(diag, axis=1, keepdims=True)
    stack[0:T] = jnp.where(ii == jj, 1.0, power)
    stack[T:] = dot(power, power)

    def double(_):
        both = dot(stack[...], stack[T:])
        stack[0:T] += both[0:T]
        stack[T:] = both[T:]

    loop(0, 4, double)

    sum_far_end(mterm, ms, mx, mx_r)
    m_near = sum_near(ms, mx, mx_s, mx_r)
    for c in m_near:
        c.start()

    for k in (1, 2):
        relay(k, wrel, wf_s, wf_r, w_dst, w_s, w_r)

    loop(0, 2, double)
    coef[...] = (stack[0:T] + dot(stack[0:T], stack[T:])) / jnp.sum(diag, axis=0, keepdims=True)

    sum_near_end(ms, mx, mx_r)
    all_send(ms, mtot, ma_s, ma_r)
    yp[...] = dot(coef[...], vp[...])
    lhs[T:] = -yp[...]
    for h in range(2):
        @pl.when(q + h * NQ <= p)
        def _():
            rhs[h, 0:T] = dot(coef[...], vc[h])

    @pl.when(q <= p)
    def _():
        got(T - S, wr_r)
        lhs[0:T] = -wp[...]

    for h in range(2):
        c = q + h * NQ

        @pl.when(c < p)
        def _():
            copy_to(rhs.at[h, pl.ds(T, T)], rhs.at[h, pl.ds(T, T)], w_s, w_r.at[h], p, q).wait_recv()

        @pl.when(c == p)
        def _():
            rhs[h, T:] = wp[...]

        @pl.when(c <= p)
        def _():
            tile = a_ref[:, h, :]
            sym = jnp.where(c < p, tile, 0.5 * (tile + tile.T))
            low[h] = sym + dot(lhs[...], rhs[h], 0, 0)

    if_any(fans, sent, w_s, 32)
    sent(2 * S, wf_s)
    if_any(others, sent, wr_s, NQ)
    sent(T - H, ga_s)
    sent(10 * H, mx_s)

    got(T - H, ma_r)
    wp[...] = dot(mtot[...] + mtot[...].T, yp[...])
    for h in range(2):
        c = q + h * NQ

        @pl.when(c <= p)
        def _():
            o_ref[:, h, :] = low[h] + dot(wp[...], rhs[h, 0:T], 0, 0)

        @pl.when(c > p)
        def _():
            o_ref[:, h, :] = jnp.zeros((T, T), f32)

    sent(T - H, ma_s)


def body(matrix, reflectors):
    vmem = lambda *shape: pltpu.VMEM(shape, f32)
    dma = lambda *shape: pltpu.SemaphoreType.DMA(shape)
    one = pltpu.SemaphoreType.DMA
    out = pl.pallas_call(
        kernel,
        out_shape=jax.ShapeDtypeStruct((T, 2, T), f32),
        in_specs=[pl.BlockSpec(memory_space=pltpu.HBM)] * 2,
        out_specs=pl.BlockSpec(memory_space=pltpu.VMEM),
        scratch_shapes=[
            vmem(T, 2, T), vmem(T, T),
            vmem(T, T), vmem(2, T, T), vmem(2, T, T), vmem(2, T, T),
            vmem(2, NQ, S, T), vmem(3, 6, S, T), vmem(3, S, T), vmem(2, S, T), vmem(NQ, S, T),
            vmem(T, T), vmem(S, T), vmem(T, T), vmem(2, S, T), vmem(2, S, T),
            vmem(S, T), vmem(3, H, T), vmem(10, H, T), vmem(T, T),
            vmem(S, T), vmem(3, H, T), vmem(10, H, T), vmem(T, T),
            vmem(2 * T, T), vmem(T, T), vmem(T, T), vmem(2 * T, T), vmem(2, 2 * T, T),
            dma(2), one, dma(2), one, dma(2), one, dma(2), one, dma(2),
            dma(2), dma(2), one, dma(3), one, one, one, one, one, one,
            one, dma(2), one, one, one, dma(2), one, one,
        ],
        compiler_params=pltpu.CompilerParams(collective_id=0, has_side_effects=True, vmem_limit_bytes=53 * 2**20),
        cost_estimate=pl.CostEstimate(flops=34 * 2 * T**3, bytes_accessed=5 * T * T * 4, transcendentals=0),
    )(matrix.reshape(T, 2, T), reflectors.reshape(T, T))
    return out.reshape(matrix.shape)


def solution(mesh):
    placed = (P(None, "prow", None, "pcol"), P(None, "prow", None))
    return jax.shard_map(
        body, mesh=mesh, in_specs=placed, out_specs=P(None, "prow", None, "pcol"), check_vma=False
    )
```
